512 devices in a mesh: dp: 16 (over y_lo, x, core), ctx: 32 (over z, y_hi).
Axes of the slice: x: 4, y: 8 (y_hi: 4, y_lo: 2; y = y_hi * 2 + y_lo), z: 8, core: 2. Of those that a mesh axis runs over, the one named last changes fastest.
Arguments:
- frames: bfloat16 [16, 4096, 1024], P('dp', 'ctx'), may hold values from -64 to 64
- cotangent: bfloat16 [16, 4096, 1024], P('dp', 'ctx'), may hold values from -200 to 200
- lengths: int32 [16, 4], P('dp'), may hold values from 1 to 2048, 4096 in all within a row
- w_query: bfloat16 [1024, 512], P('dp'), may hold values from -8 to 8
- w_key: bfloat16 [1024, 512], P('dp'), may hold values from -8 to 8
- w_value: bfloat16 [1024, 512], P('dp'), may hold values from -0.1875 to 0.1875
- w_output: bfloat16 [512, 1024], P(None, 'dp'), may hold values from -1 to 1
- att_gain: float32 [1024], replicated, may hold values from 0.25 to 1.75
- conv_gain: float32 [1024], replicated, may hold values from 0.25 to 1.75
- kernel: float32 [9, 1024], replicated, may hold values from -2 to 2
- conv_bias: float32 [1024], replicated, may hold values from -3 to 3
Outputs:
- grad_frames: float32 [16, 4096, 1024], P('dp', 'ctx')
- grad_att_gain: float32 [1024], replicated
- grad_conv_gain: float32 [1024], replicated
- grad_kernel: float32 [9, 1024], replicated
- grad_bias: float32 [1024], replicated
The draws below stay inside these ranges and needn't reach their ends.
Inputs may be any that keep to these rules, and one draw needn't show every extreme that they name: `lengths`: each row sums to 4096; its largest entry is exactly 2048.
All inputs are finite; a program needn't handle non-finite values.
Results may differ from the reference program's by a relative error of at most 0.012.
Values may be sent and summed in bfloat16 or wider, within the bound.
A program may use at most 64 MiB of HBM per device.

```python
import math
import jax
import jax.numpy as jnp
import numpy as np
from jax import lax

D = 1024
HEAD_DIM = 128
KERNEL = 9
HEADS = 4
LEFT = 128
RECS = 4
SEQS = 16
FRAMES = 4096
MOST = 2048


def draw_w_query(key, part):
    key = jax.random.fold_in(key, 21)
    own = jnp.clip(jax.random.normal(key, (D, HEADS * HEAD_DIM), jnp.float32), -6.0, 6.0) / math.sqrt(D)
    return own.astype(jnp.bfloat16)


def draw_w_key(key, part):
    key = jax.random.fold_in(key, 22)
    own = jnp.clip(jax.random.normal(key, (D, HEADS * HEAD_DIM), jnp.float32), -6.0, 6.0) / math.sqrt(D)
    return own.astype(jnp.bfloat16)


def draw_frames(key, part):
    key = jax.random.fold_in(key, 11)
    first = jax.random.fold_in(key, 0)
    second = jax.random.fold_in(key, 1)
    fourth = jax.random.fold_in(key, 3)
    column_scale = jnp.exp(jax.random.uniform(first, (D,), jnp.float32, 0.0, math.log(10.0)))
    row_scale = jnp.exp(jax.random.uniform(second, (SEQS, FRAMES, 1), jnp.float32, 0.0, math.log(10.0)))
    base = jnp.clip(jax.random.normal(fourth, (SEQS, FRAMES, D), jnp.float32), -6.0, 6.0)
    return (0.1 * base * column_scale * row_scale).astype(jnp.bfloat16)


def draw_cotangent(key, part):
    key = jax.random.fold_in(key, 12)
    second = jax.random.fold_in(key, 1)
    ramp = jnp.exp(math.log(3.0) * jnp.arange(FRAMES, dtype=jnp.float32) / max(FRAMES - 1, 1))[None, :, None]
    base = jnp.clip(jax.random.normal(second, (SEQS, FRAMES, D), jnp.float32), -6.0, 6.0)
    return (base * ramp).astype(jnp.bfloat16)


def steps_of(key, extent, cuts, low, top_value):
    factor_of, own = 1.0, jax.random.fold_in(key, 6)
    for dim, blocks in cuts:
        heights = jnp.exp(jax.random.uniform(jax.random.fold_in(own, dim), (blocks,), jnp.float32, low / len(cuts), top_value / len(cuts)))
        factor_of = factor_of * jnp.repeat(heights, extent[dim] // blocks).reshape([-1 if axis == dim else 1 for axis in range(len(extent))])
    return factor_of


def profile(count, total, bound, skew):
    loads = [(1 << 20) // math.isqrt(rank ** skew) + 1 for rank in range(2, count + 1)]
    rest, holding = total - bound - (count - 1), [1] * (count - 1)
    while rest > 0:
        free = [i for i in range(count - 1) if holding[i] < bound]
        whole, left = sum([loads[i] for i in free]), rest
        for i in free:
            addition = min(bound - holding[i], max(1, left * loads[i] // whole), rest)
            holding[i] = holding[i] + addition
            rest = rest - addition
    return np.array([bound] + holding)


def ragged(rng, amount, total, most, lean):
    if amount == 2:
        one = jax.random.randint(rng, (), max(1, total - most), min(most, total - 1) + 1)
        return jnp.stack([one, total - one])
    tallies = jnp.asarray(profile(amount, total, most, lean), jnp.int32)
    twos = (amount - 1) // 2
    giver, receiver = tallies[1:1 + 2 * twos:2], tallies[2:2 + 2 * twos:2]
    room = jnp.minimum(giver - 1, most - receiver)
    moved = jax.random.randint(jax.random.fold_in(rng, 1), (twos,), 0, 1 << 20) % (room + 1)
    tallies = tallies.at[1:1 + 2 * twos:2].set(giver - moved).at[2:2 + 2 * twos:2].set(receiver + moved)
    return tallies[jax.random.permutation(jax.random.fold_in(rng, 2), amount)]


def bell_draw(rng, dims, deviation, most, cuts=(), kind=jnp.bfloat16):
    result = jax.random.normal(rng, dims, jnp.float32) * deviation
    if len(cuts) > 0:
        result = steps_of(rng, dims, cuts, -0.22, 0.18) * result
    return jnp.clip(result, min=-most, max=most).astype(kind)


def setup_inputs(seed: int = 0) -> dict:
    arg_keys = jax.random.split(jax.random.key(seed), 12)
    return {
        "frames": draw_frames(jax.random.fold_in(arg_keys[11], 71), 0),
        "cotangent": draw_cotangent(jax.random.fold_in(arg_keys[11], 71), 0),
        "lengths": jax.vmap(lambda own: ragged(own, RECS, FRAMES, MOST, 2))(jax.random.split(arg_keys[2], SEQS)).reshape((SEQS, RECS)).astype(jnp.int32),
        "w_query": draw_w_query(jax.random.fold_in(arg_keys[11], 71), 0),
        "w_key": draw_w_key(jax.random.fold_in(arg_keys[11], 71), 0),
        "w_value": bell_draw(arg_keys[5], (D, HEADS * HEAD_DIM), D ** -0.5, 0.1875, ((0, 16),)),
        "w_output": bell_draw(arg_keys[6], (HEADS * HEAD_DIM, D), (HEADS * HEAD_DIM // 16) ** -0.5, 1.0, ((1, 16),)),
        "att_gain": jnp.clip(1.0 + 0.15 * jax.random.normal(arg_keys[7], (D,), jnp.float32), 0.25, 1.75),
        "conv_gain": jnp.clip(1.0 + 0.15 * jax.random.normal(arg_keys[8], (D,), jnp.float32), 0.25, 1.75),
        "kernel": bell_draw(arg_keys[9], (KERNEL, D), KERNEL ** -0.5, 2.0, (), jnp.float32),
        "conv_bias": bell_draw(arg_keys[10], (D,), 1.0, 3.0, (), jnp.float32),
    }


epsilon = 1e-05

def layer_norm(values, gain):
    center = values - lax.optimization_barrier(jnp.mean(values, axis=-1, keepdims=True))
    inverse = lax.rsqrt(lax.optimization_barrier(jnp.mean(center * center, axis=-1, keepdims=True)) + epsilon)
    scaled = center * inverse
    return (scaled * gain, scaled, inverse)

def norm_back(grad_out, scaled, inverse, gain):
    grad_scaled = grad_out * gain
    first = lax.optimization_barrier(jnp.mean(grad_scaled, axis=-1, keepdims=True))
    second = lax.optimization_barrier(jnp.mean(grad_scaled * scaled, axis=-1, keepdims=True))
    return (inverse * (grad_scaled - first - scaled * second), lax.optimization_barrier(jnp.sum(grad_out * scaled, axis=0)))

def segment_of(places, bounds):
    return lax.optimization_barrier(jnp.sum((bounds[None, :] <= places[:, None]).astype(jnp.int32), axis=1))

def band_mask(query_places, key_places, bounds):
    distance = query_places[:, None] - key_places[None, :]
    same = segment_of(query_places, bounds)[:, None] == segment_of(key_places, bounds)[None, :]
    return (distance >= 0) & (distance <= LEFT) & (key_places[None, :] >= 0) & same

def lift(values):
    return lax.optimization_barrier(values.astype(jnp.bfloat16)).astype(jnp.float32)

def split_heads(values):
    return values.astype(jnp.float32).reshape(values.shape[0], HEADS, HEAD_DIM)

def block_probs(query, keys, query_places, key_places, bounds):
    scores = jnp.einsum('qhd,khd->hqk', split_heads(query), split_heads(keys)) * HEAD_DIM ** (-0.5)
    allowed = band_mask(query_places, key_places, bounds)
    scores = jnp.where(allowed[None], scores, -jnp.inf)
    shifted = jnp.exp(scores - lax.optimization_barrier(jnp.max(scores, axis=-1, keepdims=True)))
    return shifted / lax.optimization_barrier(jnp.sum(shifted, axis=-1, keepdims=True))

def block_back(query, keys, values, grad_context, query_places, key_places, bounds):
    probs = block_probs(query, keys, query_places, key_places, bounds)
    heads_q = split_heads(query)
    heads_k = split_heads(keys)
    heads_g = split_heads(grad_context)
    grad_probs = jnp.einsum('qhd,khd->hqk', heads_g, split_heads(values))
    delta = lax.optimization_barrier(jnp.sum(probs * grad_probs, axis=-1, keepdims=True))
    grad_scores = lift(probs * (grad_probs - delta) * HEAD_DIM ** (-0.5))
    grad_query = jnp.einsum('hqk,khd->qhd', grad_scores, heads_k).reshape(query.shape[0], -1).astype(jnp.bfloat16)
    grad_key = jnp.einsum('hqk,qhd->khd', grad_scores, heads_q).reshape(keys.shape[0], -1)
    grad_value = jnp.einsum('hqk,qhd->khd', lift(probs), heads_g).reshape(keys.shape[0], -1)
    return (grad_query, grad_key, grad_value)

def fold_rims(parts, block):
    main = parts[:, LEFT:]
    main = main.at[:-1, block - LEFT:].add(parts[1:, :LEFT])
    return main.reshape(-1, parts.shape[-1])

def one_sequence(frames, cotangent, lengths, params):
    w_query, w_key, w_value, w_output, att_gain, conv_gain, kernel, conv_bias = params
    bounds = jnp.cumsum(lengths)
    places = jnp.arange(FRAMES, dtype=jnp.int32)
    segments = segment_of(places, bounds)
    inputs = frames.astype(jnp.float32)
    norm_a, scaled_a, inverse_a = layer_norm(inputs, att_gain)
    norm_ab = norm_a.astype(jnp.bfloat16)
    query = jnp.dot(norm_ab, w_query, preferred_element_type=jnp.float32).astype(jnp.bfloat16)
    keys = jnp.dot(norm_ab, w_key, preferred_element_type=jnp.float32).astype(jnp.bfloat16)
    values = jnp.dot(norm_ab, w_value, preferred_element_type=jnp.float32).astype(jnp.bfloat16)
    heads_width = query.shape[1]
    block = math.gcd(FRAMES, 512)
    count = FRAMES // block
    span = block + LEFT
    padding = jnp.zeros((LEFT, heads_width), jnp.bfloat16)
    keys_pad = jnp.concatenate([padding, keys], axis=0)
    values_pad = jnp.concatenate([padding, values], axis=0)

    def pieces(index):
        first = (index * block).astype(jnp.int32)
        query_rows = lax.dynamic_slice_in_dim(query, first, block, 0)
        key_rows = lax.dynamic_slice_in_dim(keys_pad, first, span, 0)
        value_rows = lax.dynamic_slice_in_dim(values_pad, first, span, 0)
        query_places = first + jnp.arange(block, dtype=jnp.int32)
        key_places = first - LEFT + jnp.arange(span, dtype=jnp.int32)
        return (first, query_rows, key_rows, value_rows, query_places, key_places)

    def forward_block(index):
        first, query_rows, key_rows, value_rows, query_places, key_places = pieces(index)
        probs = block_probs(query_rows, key_rows, query_places, key_places, bounds)
        context = jnp.einsum('hqk,khd->qhd', lift(probs), split_heads(value_rows))
        return context.reshape(block, heads_width).astype(jnp.bfloat16)
    blocks = jnp.arange(count, dtype=jnp.int32)
    context = lax.map(forward_block, blocks).reshape(FRAMES, heads_width)
    mid = inputs + jnp.dot(context, w_output, preferred_element_type=jnp.float32)
    norm_c, scaled_c, inverse_c = layer_norm(mid, conv_gain)
    conv_in = norm_c.astype(jnp.bfloat16)
    conv_pad = jnp.concatenate([jnp.zeros((KERNEL - 1, D), jnp.bfloat16), conv_in], axis=0)
    conv = jnp.zeros((FRAMES, D), jnp.float32) + conv_bias
    tap_masks = []
    for tap in range(KERNEL):
        sources = places - KERNEL + 1 + tap
        valid = ((sources >= 0) & (segment_of(sources, bounds) == segments))[:, None]
        tap_masks.append(valid)
        conv = conv + jnp.where(valid, kernel[tap] * conv_pad[tap:tap + FRAMES].astype(jnp.float32), 0.0)
    grad_out = cotangent.astype(jnp.float32)
    gate_value = jax.nn.sigmoid(conv)
    grad_conv = grad_out * gate_value * (1.0 + conv * (1.0 - gate_value))
    grad_bias = lax.optimization_barrier(jnp.sum(grad_conv, axis=0))
    kernel_rows = []
    grad_pad = jnp.zeros((FRAMES + KERNEL - 1, D), jnp.float32)
    for tap in range(KERNEL):
        kept = jnp.where(tap_masks[tap], grad_conv, 0.0)
        kernel_rows.append(lax.optimization_barrier(jnp.sum(kept * conv_pad[tap:tap + FRAMES].astype(jnp.float32), axis=0)))
        grad_pad = grad_pad + jnp.pad(kernel[tap] * kept, ((tap, KERNEL - 1 - tap), (0, 0)))
    grad_kernel = jnp.stack(kernel_rows)
    grad_conv_in = grad_pad[KERNEL - 1:]
    grad_mid_norm, grad_conv_gain = norm_back(grad_conv_in, scaled_c, inverse_c, conv_gain)
    grad_mid = grad_out + grad_mid_norm
    grad_mid_b = grad_mid.astype(jnp.bfloat16)
    grad_context = jnp.dot(grad_mid_b, w_output.T, preferred_element_type=jnp.float32).astype(jnp.bfloat16)

    def backward_block(index):
        first, query_rows, key_rows, value_rows, query_places, key_places = pieces(index)
        grad_rows = lax.dynamic_slice_in_dim(grad_context, first, block, 0)
        return block_back(query_rows, key_rows, value_rows, grad_rows, query_places, key_places, bounds)
    grad_query, grad_key_parts, grad_value_parts = lax.map(backward_block, blocks)
    grad_query = grad_query.reshape(FRAMES, heads_width)
    grad_key = fold_rims(grad_key_parts, block).astype(jnp.bfloat16)
    grad_value = fold_rims(grad_value_parts, block).astype(jnp.bfloat16)
    grad_norm_a = jnp.dot(grad_query, w_query.T, preferred_element_type=jnp.float32)
    grad_norm_a = grad_norm_a + jnp.dot(grad_key, w_key.T, preferred_element_type=jnp.float32)
    grad_norm_a = grad_norm_a + jnp.dot(grad_value, w_value.T, preferred_element_type=jnp.float32)
    grad_input_norm, grad_att_gain = norm_back(grad_norm_a, scaled_a, inverse_a, att_gain)
    grad_frames = grad_mid_norm + grad_input_norm
    return (grad_frames, grad_att_gain, grad_conv_gain, grad_kernel, grad_bias)

def reference(frames, cotangent, lengths, w_query, w_key, w_value, w_output, att_gain, conv_gain, kernel, conv_bias):
    params = (w_query, w_key, w_value, w_output, att_gain, conv_gain, kernel, conv_bias)

    def per_sequence(item):
        return one_sequence(item[0], item[1], item[2], params)
    grad_frames, gains_a, gains_c, kernels, biases = lax.map(per_sequence, (frames, cotangent, lengths))
    factor = 1.0 / math.sqrt(SEQS * FRAMES)
    return (grad_frames, lax.optimization_barrier(jnp.sum(gains_a, axis=0)) * factor, lax.optimization_barrier(jnp.sum(gains_c, axis=0)) * factor, lax.optimization_barrier(jnp.sum(kernels, axis=0)) * factor, lax.optimization_barrier(jnp.sum(biases, axis=0)) * factor)
```

```python
import math

import jax
import jax.numpy as jnp
from jax import lax
from jax.experimental import pallas as pl
from jax.experimental.pallas import tpu as pltpu
from jax.sharding import PartitionSpec as P

MESH = pl.DeviceIdType.MESH
NX, NY, NZ = 4, 8, 8
ROWS = 128
WIDTH = 1024
HEADS = 4
HEAD_DIM = 128
HEADS_WIDTH = HEADS * HEAD_DIM
LEFT = 128
TAPS = 9
RIM = 16
EXT = 2 * ROWS + 2 * RIM
CONV = ROWS + 16
DEEP = 64
GROUP = 8
EPSILON = 1e-05
FAR = -1e30
BEFORE = -(1 << 20)
SCALE = HEAD_DIM ** (-0.5)
SLOTS = 176
F32 = jnp.float32
BF16 = jnp.bfloat16

SHARDS = ((-1, 0), (1, 0), (2, 0), (0, 1), (-1, 1), (1, 1), (2, 1))


class Links:
    def __init__(self, send_sems, recv_sems):
        self.send_sems, self.recv_sems = send_sems, recv_sems
        self.names, self.sent = {}, []

    def copy(self, name, source, target, device):
        slot = self.names.setdefault(name, len(self.names))
        assert slot < SLOTS
        return pltpu.make_async_remote_copy(
            src_ref=source,
            dst_ref=target,
            send_sem=self.send_sems.at[slot],
            recv_sem=self.recv_sems.at[slot],
            device_id=device,
            device_id_type=MESH,
        )

    def send(self, name, source, target, device):
        copy = self.copy(name, source, target, device)
        copy.start()
        self.sent.append(copy)

    def arrived(self, name, target, device):
        self.copy(name, target, target, device).wait_recv()

    def finish(self):
        for copy in self.sent:
            copy.wait_send()


def dot(left, right):
    return jnp.dot(left, right, preferred_element_type=F32)


def dot_nt(left, right):
    return lax.dot_general(left, right, (((1,), (1,)), ((), ())), preferred_element_type=F32)


def dot_tn(left, right):
    return lax.dot_general(left, right, (((0,), (0,)), ((), ())), preferred_element_type=F32)


def normalize(values):
    center = values - jnp.mean(values, axis=-1, keepdims=True)
    inverse = lax.rsqrt(jnp.mean(center * center, axis=-1, keepdims=True) + EPSILON)
    return center * inverse, inverse


def wide(column, width):
    return jnp.broadcast_to(column, (column.shape[0], width))


def spread(block):
    return jnp.concatenate([block] * (WIDTH // 128), axis=1)


def iota(shape, axis):
    return lax.broadcasted_iota(jnp.int32, shape, axis)


def block_kernel(
    frames, cotangent, lengths, w_query, w_key, w_value, w_output, att_gain, conv_gain, kernel, bias,
    out_frames, out_att, out_conv, out_kernel, out_bias,
    xs, cts, weights, w_in, gain_a, gain_c, taps_ref, bias_ref,
    norm_b, scaled_a, inverse_a, keys, values, query, query_e, query_n, probs, context, mid,
    scaled_c, inverse_c, conv_in, age, grad_conv, grad_conv_in, grad_mid_norm, grad_mid_b,
    grad_context, grad_context_n, grad_query, grad_key, grad_value, grad_key_f, grad_value_f, grad_norm_a,
    frames_out, mask_main, mask_rim, mask_next, stats, stats_n, delta, delta_n,
    early, early_x, early_y, early_z, early_all, late_sum, late_x, late_y, late_z,
    att_row, conv_row, kernel_rows, bias_row,
    send_sems, recv_sems, local_sems,
):
    dp, ctx = lax.axis_index("dp"), lax.axis_index("ctx")
    core = lax.rem(dp, 2)
    x = lax.rem(lax.div(dp, 2), NX)
    y_lo = lax.div(dp, 2 * NX)
    z = lax.div(ctx, NY // 2)
    y = lax.rem(ctx, NY // 2) * 2 + y_lo
    offset = ctx * ROWS
    group = x * 2 + core

    def at(px, py, pz, pc):
        return ((lax.rem(py, 2) * NX + px) * 2 + pc, pz * (NY // 2) + lax.div(py, 2))

    def shift(value, step, size):
        return lax.rem(value + (step + size), size)

    def frames_at(step):
        return (dp, shift(ctx, step, 4 * NZ))

    sibling = (dp + 1 - 2 * core, ctx)
    right, left = at(shift(x, 1, NX), y, z, core), at(shift(x, -1, NX), y, z, core)
    above, below = at(x, shift(y, 1, NY), z, core), at(x, shift(y, -1, NY), z, core)
    front, back = at(x, y, shift(z, 1, NZ), core), at(x, y, shift(z, -1, NZ), core)
    later, earlier, later_2 = frames_at(1), frames_at(-1), frames_at(2)

    def group_peer(step):
        other = shift(group, step, GROUP)
        return other, at(lax.div(other, 2), y, z, lax.rem(other, 2))

    def y_peer(step):
        other = shift(y, step, NY)
        return other, at(x, other, z, core)

    def z_peer(step):
        other = shift(z, step, NZ)
        return other, at(x, y, other, core)

    links = Links(send_sems, recv_sems)
    local = []

    def bring(source, target):
        copy = pltpu.make_async_copy(source, target, local_sems.at[len(local)])
        copy.start()
        local.append(copy)
        return copy

    own_rows = pl.ds(pl.multiple_of(dp * DEEP, DEEP), DEEP)
    got_output = bring(w_output, w_in)
    got_weights = [
        bring(source, weights.at[index, own_rows, :])
        for index, source in ((0, w_key), (1, w_value), (2, w_query))
    ]
    got_frames = bring(frames.at[0], xs.at[pl.ds(0, ROWS), :])
    got_rest = [
        bring(cotangent.at[0], cts.at[pl.ds(0, ROWS), :]),
        bring(att_gain, gain_a),
        bring(conv_gain, gain_c),
        bring(kernel, taps_ref),
        bring(bias, bias_ref),
    ]

    barrier = pltpu.get_barrier_semaphore()
    peers = [group_peer(step)[1] for step in range(1, GROUP)]
    peers += [y_peer(step)[1] for step in range(1, NY)]
    peers += [z_peer(step)[1] for step in range(1, NZ)]
    peers += [later, earlier, later_2, frames_at(-2)]
    for peer in peers:
        pl.semaphore_signal(barrier, inc=1, device_id=peer, device_id_type=MESH)
    got_output.wait()
    weights[3, own_rows, :] = w_in[...].astype(F32).T.astype(BF16)
    for copy in got_weights:
        copy.wait()
    pl.semaphore_wait(barrier, len(peers))

    links.send("prev", frames.at[0], xs.at[pl.ds(ROWS, ROWS), :], later)
    links.send("next", frames.at[0, pl.ds(0, RIM), :], xs.at[pl.ds(2 * ROWS + RIM, RIM), :], earlier)
    links.send("prev2", frames.at[0, pl.ds(ROWS - RIM, RIM), :], xs.at[pl.ds(2 * ROWS, RIM), :], later_2)
    links.send("cot", cotangent.at[0, pl.ds(0, RIM), :], cts.at[pl.ds(ROWS, RIM), :], earlier)

    half = lax.rem(z, 2)

    def shard(index, of_core):
        if index is None:
            return (y_lo * NX + x) * 2 + of_core
        step, other = SHARDS[index]
        side = 1 - y_lo if other else y_lo
        return (side * NX + shift(x, step, NX)) * 2 + of_core

    def piece(index, of_half, part, wave, of_core):
        first, size = shard(index, of_core) * DEEP, DEEP
        if of_half is not None:
            first, size = first + of_half * 32, 32
        if part is not None:
            first, size = first + part * 16, 16
        return weights.at[pl.ds(2 * wave, 2), pl.ds(pl.multiple_of(first, 16), size), :]

    def give(name, index, of_half, part, wave, device):
        ref = piece(index, of_half, part, wave, core)
        links.send((name, wave), ref, ref, device)

    def take(name, index, of_half, part, wave, of_core=None):
        ref = piece(index, of_half, part, wave, core if of_core is None else of_core)
        links.arrived((name, wave), ref, sibling)

    siblings = []

    def pass_on(name, index, of_half, part, wave):
        give("sib" + name, index, of_half, part, wave, sibling)
        siblings.append((name, index, of_half, part, wave))

    def pass_z(index, parts, wave):
        for part in parts:
            give(f"z{part}{index}", index, half, part, wave, (front, back)[part])

    for wave in (0, 1):
        give("0", None, half, None, wave, right)
        give("1", None, half, None, wave, left)
        give("3", None, half, None, wave, below)
        pass_on("own", None, None, None, wave)

    got_frames.wait()
    for copy in got_rest:
        copy.wait()

    def norm_rows(first, size, own):
        block = xs[pl.ds(first, size), :].astype(F32)
        scaled, inverse = normalize(block)
        norm_b[pl.ds(first, size), :] = (scaled * gain_a[...]).astype(BF16)
        if own:
            scaled_a[pl.ds(first, size), :] = scaled
            inverse_a[pl.ds(first, size), :] = wide(inverse, 128)
            mid[pl.ds(pl.multiple_of(first + 8, 8), size), :] = block
        return block

    @pl.loop(0, 4)
    def _(step):
        norm_rows(pl.multiple_of(step * 32, 32), 32, True)

    ends = [jnp.int32(0)]
    for record in range(lengths.shape[1]):
        ends.append(ends[-1] + lengths[0, record])

    def start_of(places):
        start = jnp.full(places.shape, BEFORE, jnp.int32)
        for end in ends:
            start = jnp.where(places >= end, end, start)
        return start

    def mask_of(query_places, key_places):
        first = jnp.maximum(start_of(query_places), query_places - LEFT)
        return jnp.where((key_places <= query_places) & (key_places >= first), 0.0, FAR).astype(F32)

    square = (ROWS, ROWS)
    place_rows, place_lanes = offset + iota(square, 0), offset + iota(square, 1)
    mask_main[:, :ROWS] = mask_of(place_rows, place_lanes)
    mask_main[:, ROWS:] = mask_of(place_rows, place_lanes - ROWS)
    mask_next[...] = mask_of(place_lanes + ROWS, place_rows)
    rim_rows = iota((16, EXT), 0)
    rim_places = offset + jnp.where(rim_rows < 8, rim_rows - 8, rim_rows + (ROWS - 8))
    lanes = iota((16, EXT), 1)
    rim_keys = jnp.where(lanes < ROWS, lanes, lanes - 2 * ROWS)
    rim_keys = jnp.where(lanes < 2 * ROWS, rim_keys, lanes - (3 * ROWS + RIM))
    rim_keys = offset + jnp.where(lanes < 2 * ROWS + RIM, rim_keys, lanes - (ROWS + RIM))
    mask_rim[...] = mask_of(rim_places, rim_keys)
    age_rows = offset + iota((ROWS + 8, 128), 0)
    age[...] = age_rows - start_of(age_rows)

    for wave in (0, 1):
        take("0", 0, half, None, wave)
        give("20", 0, half, 0, wave, right)
        take("1", 1, half, None, wave)
        give("21", 1, half, 1, wave, left)
        take("3", 3, half, None, wave)
        give("4", 3, half, None, wave, right)
        give("5", 3, half, None, wave, left)
        for index in (0, 1, 3):
            pass_z(index, (0, 1), wave)
            pass_on(str(index), index, half, None, wave)
    for wave in (0, 1):
        take("4", 4, half, None, wave)
        give("60", 4, half, 0, wave, right)
        take("5", 5, half, None, wave)
        give("61", 5, half, 1, wave, left)
        for part in (0, 1):
            take(f"2{part}", 2, half, part, wave)
            pass_z(2, (part,), wave)
            pass_on(f"2{part}", 2, half, part, wave)
        for index in (4, 5):
            pass_z(index, (0, 1), wave)
            pass_on(str(index), index, half, None, wave)
    for wave in (0, 1):
        for part in (0, 1):
            take(f"6{part}", 6, half, part, wave)
            pass_z(6, (part,), wave)
            pass_on(f"6{part}", 6, half, part, wave)
        for index in (0, 1, 3, 2, 4, 5, 6):
            for part in (0, 1):
                take(f"z{part}{index}", index, 1 - half, part, wave)
                pass_on(f"z{part}{index}", index, 1 - half, part, wave)

    links.arrived("prev", xs.at[pl.ds(ROWS, ROWS), :], earlier)
    links.arrived("next", xs.at[pl.ds(2 * ROWS + RIM, RIM), :], earlier)
    links.arrived("prev2", xs.at[pl.ds(2 * ROWS, RIM), :], earlier)
    links.arrived("cot", cts.at[pl.ds(ROWS, RIM), :], earlier)

    @pl.loop(4, 8)
    def _(step):
        norm_rows(pl.multiple_of(step * 32, 32), 32, False)

    block = norm_rows(2 * ROWS, 2 * RIM, False)
    mid[pl.ds(ROWS + 8, 8), :] = block[RIM : RIM + 8]
    mid[pl.ds(0, 8), :] = xs[pl.ds(2 * ROWS - RIM, RIM), :].astype(F32)[8:]

    for name, index, of_half, part, wave in siblings:
        take("sib" + name, index, of_half, part, wave, 1 - core)

    normed = norm_b[...]
    keys[...] = dot(normed, weights[0]).astype(BF16)
    values[...] = dot(normed, weights[1]).astype(BF16)
    rows = jnp.concatenate(
        [normed[:ROWS], normed[2 * ROWS - RIM : 2 * ROWS], normed[2 * ROWS + RIM :]], axis=0
    )
    projected = dot(rows, weights[2])
    query[...] = projected[:ROWS].astype(BF16)
    query_e[...] = projected[ROWS + 8 : ROWS + 24].astype(BF16)
    links.send("query", query, query_n, earlier)

    def head(index):
        return slice(index * HEAD_DIM, (index + 1) * HEAD_DIM)

    lane = iota(square, 1)
    columns = jnp.zeros(square, F32)
    for h in range(HEADS):
        scores = dot_nt(query[:, head(h)], keys[: 2 * ROWS, head(h)]) * SCALE + mask_main[...]
        top = jnp.max(scores, axis=-1, keepdims=True)
        shifted = jnp.exp(scores - top)
        part = 1.0 / jnp.sum(shifted, axis=-1, keepdims=True)
        share = shifted * part
        probs[h] = share
        context[8 : ROWS + 8, head(h)] = dot(share.astype(BF16), values[: 2 * ROWS, head(h)])
        columns = jnp.where(lane == h, top, columns)
        columns = jnp.where(lane == HEADS + h, part, columns)
        scores = dot_nt(query_e[:, head(h)], keys[:, head(h)]) * SCALE + mask_rim[...]
        shifted = jnp.exp(scores - jnp.max(scores, axis=-1, keepdims=True))
        share = shifted * (1.0 / jnp.sum(shifted, axis=-1, keepdims=True))
        rims = dot(share.astype(BF16), values[:, head(h)])
        context[0:8, head(h)] = rims[:8]
        context[ROWS + 8 :, head(h)] = rims[8:]
    stats[...] = columns.T[:8]
    links.send("stats", stats, stats_n, earlier)

    mid[...] += dot_nt(context[...].astype(BF16), weights[3])

    @pl.loop(0, 3)
    def _(step):
        part_rows = pl.ds(pl.multiple_of(step * 48, 8), 48)
        scaled, inverse = normalize(mid[part_rows, :])
        scaled_c[part_rows, :] = scaled
        inverse_c[part_rows, :] = wide(inverse, 128)
        normed = (scaled * gain_c[...]).astype(BF16).astype(F32)
        for tile in range(WIDTH // 128):
            conv_in[tile, part_rows, :] = normed[:, tile * 128 : (tile + 1) * 128]

    @pl.loop(0, WIDTH // 128)
    def _(tile):
        part_lanes = pl.ds(pl.multiple_of(tile * 128, 128), 128)
        conv = jnp.broadcast_to(bias_ref[:, part_lanes], (ROWS + 8, 128))
        for back_by in range(TAPS):
            term = conv_in[tile, pl.ds(8 - back_by, ROWS + 8), :]
            term = term * taps_ref[TAPS - 1 - back_by : TAPS - back_by, part_lanes]
            conv = conv + jnp.where(age[...] >= back_by, term, 0.0)
        gate = 1.0 / (1.0 + jnp.exp(-conv))
        grad_out = cts[:, part_lanes].astype(F32)[: ROWS + 8]
        grad = grad_out * gate * (1.0 + conv * (1.0 - gate))
        grad_conv[...] = grad
        grad = grad[:ROWS]
        early[tile, 9:10, :] = jnp.sum(grad, axis=0, keepdims=True)
        total = jnp.zeros((ROWS, 128), F32)
        for back_by in range(TAPS):
            tap = TAPS - 1 - back_by
            kept = jnp.where(age[:ROWS, :] >= back_by, grad, 0.0)
            term = kept * conv_in[tile, pl.ds(8 - back_by, ROWS), :]
            early[tile, tap : tap + 1, :] = jnp.sum(term, axis=0, keepdims=True)
            ahead = pl.ds(back_by, ROWS)
            kept = jnp.where(age[ahead, :] >= back_by, grad_conv[ahead, :], 0.0)
            total = total + kept * taps_ref[tap : tap + 1, part_lanes]
        grad_conv_in[:, part_lanes] = total
        term = total * scaled_c[8 : ROWS + 8, part_lanes]
        early[tile, 10:11, :] = jnp.sum(term, axis=0, keepdims=True)
        early[tile, 11:16, :] = jnp.zeros((5, 128), F32)

    def collect(name, me, size, slots):
        for step in range(1, size):
            links.arrived((name, step), slots.at[shift(me, -step, size)], sibling)
        total = slots[0]
        for index in range(1, size):
            total = total + slots[index]
        return total

    early_x[group] = early[group]
    for step in range(1, GROUP):
        other, device = group_peer(step)
        links.send(("ex", step), early.at[other], early_x.at[group], device)

    @pl.loop(0, 4)
    def _(step):
        part_rows = pl.ds(pl.multiple_of(step * 32, 32), 32)
        ext_rows = pl.ds(pl.multiple_of(step * 32 + 8, 8), 32)
        grad, scaled = grad_conv_in[part_rows, :] * gain_c[...], scaled_c[ext_rows, :]
        first = jnp.mean(grad, axis=-1, keepdims=True)
        second = jnp.mean(grad * scaled, axis=-1, keepdims=True)
        result = spread(inverse_c[ext_rows, :]) * (grad - first - scaled * second)
        grad_mid_norm[part_rows, :] = result
        grad_mid_b[part_rows, :] = (cts[part_rows, :].astype(F32) + result).astype(BF16)

    grad_context[...] = dot(grad_mid_b[...], weights[3]).astype(BF16)
    links.send("grad", grad_context, grad_context_n, earlier)
    columns = jnp.zeros(square, F32)
    deltas = []
    for h in range(HEADS):
        term = context[8 : ROWS + 8, head(h)] * grad_context[:, head(h)].astype(F32)
        deltas.append(jnp.sum(term, axis=-1, keepdims=True))
        columns = jnp.where(lane == h, deltas[h], columns)
    delta[...] = columns.T[:8]
    links.send("delta", delta, delta_n, earlier)

    early_y[y] = collect("ex", group, GROUP, early_x)
    for step in range(1, NY):
        links.send(("ey", step), early_y.at[y], early_y.at[y], y_peer(step)[1])

    for h in range(HEADS):
        grad_h = grad_context[:, head(h)]
        share = probs[h]
        grad_probs = dot_nt(grad_h, values[: 2 * ROWS, head(h)])
        grad_scores = (share * (grad_probs - deltas[h]) * SCALE).astype(BF16)
        grad_query[:, head(h)] = dot(grad_scores, keys[: 2 * ROWS, head(h)]).astype(BF16)
        grad_key_f[:, head(h)] = dot_tn(grad_scores[:, :ROWS], query[:, head(h)])
        grad_value_f[:, head(h)] = dot_tn(share[:, :ROWS].astype(BF16), grad_h)

    early_z[z] = collect("ey", y, NY, early_y)
    for step in range(1, NZ):
        links.send(("ez", step), early_z.at[z], early_z.at[z], z_peer(step)[1])
    grad_norm_a[...] = dot_nt(grad_query[...], weights[2])

    links.arrived("query", query_n, earlier)
    links.arrived("stats", stats_n, earlier)
    links.arrived("grad", grad_context_n, earlier)
    links.arrived("delta", delta_n, earlier)
    for h in range(HEADS):
        query_h, grad_h = query_n[:, head(h)], grad_context_n[:, head(h)]
        scores = dot_nt(keys[:ROWS, head(h)], query_h) * SCALE + mask_next[...]
        share = jnp.exp(scores - stats_n[h : h + 1, :]) * stats_n[HEADS + h : HEADS + h + 1, :]
        grad_probs = dot_nt(values[:ROWS, head(h)], grad_h)
        grad_scores = (share * (grad_probs - delta_n[h : h + 1, :]) * SCALE).astype(BF16)
        total = grad_key_f[:, head(h)] + dot(grad_scores, query_h)
        grad_key[:, head(h)] = total.astype(BF16)
        total = grad_value_f[:, head(h)] + dot(share.astype(BF16), grad_h)
        grad_value[:, head(h)] = total.astype(BF16)

    early_all[group] = collect("ez", z, NZ, early_z)
    for step in range(1, GROUP):
        links.send(("ea", step), early_all.at[group], early_all.at[group], group_peer(step)[1])

    grad_norm_a[...] += dot_nt(grad_key[...], weights[0]) + dot_nt(grad_value[...], weights[1])

    product = grad_norm_a[...] * scaled_a[...]
    total = jnp.sum(product, axis=0, keepdims=True)
    for tile in range(WIDTH // 128):
        late_sum[tile : tile + 1, :] = total[:, tile * 128 : (tile + 1) * 128]
    late_x[group] = late_sum[...]
    for step in range(1, GROUP):
        links.send(("lx", step), late_x.at[group], late_x.at[group], group_peer(step)[1])

    @pl.loop(0, 4)
    def _(step):
        part_rows = pl.ds(pl.multiple_of(step * 32, 32), 32)
        grad, scaled = grad_norm_a[part_rows, :] * gain_a[...], scaled_a[part_rows, :]
        first = jnp.mean(grad, axis=-1, keepdims=True)
        second = jnp.mean(grad * scaled, axis=-1, keepdims=True)
        result = spread(inverse_a[part_rows, :]) * (grad - first - scaled * second)
        frames_out[part_rows, :] = grad_mid_norm[part_rows, :] + result

    out_copies = [bring(frames_out, out_frames.at[0])]

    late_y[y] = collect("lx", group, GROUP, late_x)
    for step in range(1, NY):
        links.send(("ly", step), late_y.at[y], late_y.at[y], y_peer(step)[1])

    factor = 1.0 / math.sqrt(NX * 2 * 2 * (NY // 2) * NZ * ROWS)
    for step in range(1, GROUP):
        links.arrived(("ea", step), early_all.at[shift(group, -step, GROUP)], sibling)
    for tile in range(WIDTH // 128):
        part_lanes = slice(tile * 128, (tile + 1) * 128)
        summed = early_all[tile] * factor
        kernel_rows[:, part_lanes] = summed[:TAPS]
        bias_row[:, part_lanes] = summed[9:10]
        conv_row[:, part_lanes] = summed[10:11]
    out_copies.append(bring(kernel_rows, out_kernel))
    out_copies.append(bring(bias_row, out_bias))
    out_copies.append(bring(conv_row, out_conv))

    late_z[z] = collect("ly", y, NY, late_y)
    for step in range(1, NZ):
        links.send(("lz", step), late_z.at[z], late_z.at[z], z_peer(step)[1])
    links.finish()
    summed = collect("lz", z, NZ, late_z) * factor
    for tile in range(WIDTH // 128):
        att_row[:, tile * 128 : (tile + 1) * 128] = summed[tile : tile + 1]
    out_copies.append(bring(att_row, out_att))
    for copy in out_copies:
        copy.wait()


def scratch():
    def buffer(*shape, dtype=F32):
        return pltpu.VMEM(shape, dtype)

    return [
        buffer(EXT, WIDTH, dtype=BF16),
        buffer(CONV, WIDTH, dtype=BF16),
        buffer(4, WIDTH, HEADS_WIDTH, dtype=BF16),
        buffer(HEADS_WIDTH, DEEP, dtype=BF16),
        buffer(1, WIDTH),
        buffer(1, WIDTH),
        buffer(TAPS, WIDTH),
        buffer(1, WIDTH),
        buffer(EXT, WIDTH, dtype=BF16),
        buffer(ROWS, WIDTH),
        buffer(ROWS, 128),
        buffer(EXT, HEADS_WIDTH, dtype=BF16),
        buffer(EXT, HEADS_WIDTH, dtype=BF16),
        buffer(ROWS, HEADS_WIDTH, dtype=BF16),
        buffer(16, HEADS_WIDTH, dtype=BF16),
        buffer(ROWS, HEADS_WIDTH, dtype=BF16),
        buffer(HEADS, ROWS, 2 * ROWS),
        buffer(CONV, HEADS_WIDTH),
        buffer(CONV, WIDTH),
        buffer(CONV, WIDTH),
        buffer(CONV, 128),
        buffer(WIDTH // 128, CONV, 128),
        buffer(ROWS + 8, 128, dtype=jnp.int32),
        buffer(ROWS + 8, 128),
        buffer(ROWS, WIDTH),
        buffer(ROWS, WIDTH),
        buffer(ROWS, WIDTH, dtype=BF16),
        buffer(ROWS, HEADS_WIDTH, dtype=BF16),
        buffer(ROWS, HEADS_WIDTH, dtype=BF16),
        buffer(ROWS, HEADS_WIDTH, dtype=BF16),
        buffer(ROWS, HEADS_WIDTH, dtype=BF16),
        buffer(ROWS, HEADS_WIDTH, dtype=BF16),
        buffer(ROWS, HEADS_WIDTH),
        buffer(ROWS, HEADS_WIDTH),
        buffer(ROWS, WIDTH),
        buffer(ROWS, WIDTH),
        buffer(ROWS, 2 * ROWS),
        buffer(16, EXT),
        buffer(ROWS, ROWS),
        buffer(8, 128),
        buffer(8, 128),
        buffer(8, 128),
        buffer(8, 128),
        buffer(GROUP, 16, 128),
        buffer(GROUP, 16, 128),
        buffer(NY, 16, 128),
        buffer(NZ, 16, 128),
        buffer(GROUP, 16, 128),
        buffer(8, 128),
        buffer(GROUP, 8, 128),
        buffer(NY, 8, 128),
        buffer(NZ, 8, 128),
        buffer(1, WIDTH),
        buffer(1, WIDTH),
        buffer(TAPS, WIDTH),
        buffer(1, WIDTH),
        pltpu.SemaphoreType.DMA((SLOTS,)),
        pltpu.SemaphoreType.DMA((SLOTS,)),
        pltpu.SemaphoreType.DMA((16,)),
    ]


def shards(
    frames, cotangent, lengths, w_query, w_key, w_value, w_output, att_gain, conv_gain, kernel, conv_bias
):
    row = (1, WIDTH)
    anywhere = pl.BlockSpec(memory_space=pl.ANY)
    in_specs = [anywhere] * 11
    in_specs[2] = pl.BlockSpec(memory_space=pltpu.SMEM)
    result = pl.pallas_call(
        block_kernel,
        out_shape=(
            jax.ShapeDtypeStruct(frames.shape, F32),
            jax.ShapeDtypeStruct(row, F32),
            jax.ShapeDtypeStruct(row, F32),
            jax.ShapeDtypeStruct(kernel.shape, F32),
            jax.ShapeDtypeStruct(row, F32),
        ),
        in_specs=in_specs,
        out_specs=(anywhere,) * 5,
        scratch_shapes=scratch(),
        compiler_params=pltpu.CompilerParams(
            collective_id=0, has_side_effects=True, vmem_limit_bytes=48 << 20
        ),
        cost_estimate=pl.CostEstimate(
            flops=3 << 30, bytes_accessed=4 << 20, transcendentals=1 << 20
        ),
    )(
        frames, cotangent, lengths, w_query, w_key, w_value, w_output,
        att_gain.reshape(row), conv_gain.reshape(row), kernel, conv_bias.reshape(row),
    )
    grad_frames, grad_att, grad_conv, grad_kernel, grad_bias = result
    return (
        grad_frames,
        grad_att.reshape(WIDTH),
        grad_conv.reshape(WIDTH),
        grad_kernel,
        grad_bias.reshape(WIDTH),
    )


def solution(mesh):
    return jax.shard_map(
        shards,
        mesh=mesh,
        in_specs=(
            P("dp", "ctx", None),
            P("dp", "ctx", None),
            P("dp", None),
            P("dp", None),
            P("dp", None),
            P("dp", None),
            P(None, "dp"),
            P(),
            P(),
            P(),
            P(),
        ),
        out_specs=(P("dp", "ctx", None), P(), P(), P(), P()),
        check_vma=False,
    )
```

```python
import math

import jax
import jax.numpy as jnp
from jax import lax
from jax.experimental import pallas as pl
from jax.experimental.pallas import tpu as pltpu
from jax.sharding import PartitionSpec as P

MESH = pl.DeviceIdType.MESH
NX, NY, NZ = 4, 8, 8
ROWS = 128
WIDTH = 1024
HEADS = 4
HEAD_DIM = 128
HEADS_WIDTH = HEADS * HEAD_DIM
LEFT = 128
TAPS = 9
RIM = 16
EXT = 2 * ROWS + 2 * RIM
CONV = ROWS + 16
DEEP = 64
GROUP = 8
EPSILON = 1e-05
FAR = -1e30
BEFORE = -(1 << 20)
SCALE = HEAD_DIM ** (-0.5)
SLOTS = 176
F32 = jnp.float32
BF16 = jnp.bfloat16

SHARDS = ((-1, 0), (1, 0), (2, 0), (0, 1), (-1, 1), (1, 1), (2, 1))


class Links:
    def __init__(self, send_sems, recv_sems):
        self.send_sems, self.recv_sems = send_sems, recv_sems
        self.names, self.sent = {}, []

    def copy(self, name, source, target, device):
        slot = self.names.setdefault(name, len(self.names))
        assert slot < SLOTS
        return pltpu.make_async_remote_copy(
            src_ref=source,
            dst_ref=target,
            send_sem=self.send_sems.at[slot],
            recv_sem=self.recv_sems.at[slot],
            device_id=device,
            device_id_type=MESH,
        )

    def send(self, name, source, target, device):
        copy = self.copy(name, source, target, device)
        copy.start()
        self.sent.append(copy)

    def arrived(self, name, target, device):
        self.copy(name, target, target, device).wait_recv()

    def finish(self):
        for copy in self.sent:
            copy.wait_send()


def dot(left, right):
    return jnp.dot(left, right, preferred_element_type=F32)


def dot_nt(left, right):
    return lax.dot_general(left, right, (((1,), (1,)), ((), ())), preferred_element_type=F32)


def dot_tn(left, right):
    return lax.dot_general(left, right, (((0,), (0,)), ((), ())), preferred_element_type=F32)


def normalize(values):
    center = values - jnp.mean(values, axis=-1, keepdims=True)
    inverse = lax.rsqrt(jnp.mean(center * center, axis=-1, keepdims=True) + EPSILON)
    return center * inverse, inverse


def wide(column, width):
    return jnp.broadcast_to(column, (column.shape[0], width))


def spread(block):
    return jnp.concatenate([block] * (WIDTH // 128), axis=1)


def iota(shape, axis):
    return lax.broadcasted_iota(jnp.int32, shape, axis)


def block_kernel(
    frames, cotangent, lengths, w_query, w_key, w_value, w_output, att_gain, conv_gain, kernel, bias,
    out_frames, out_sums,
    xs, cts, weights, gain_a, gain_c, taps_ref, bias_ref,
    norm_b, scaled_a, inverse_a, keys, values, query, query_e, query_n, probs, context, mid,
    scaled_c, inverse_c, conv_in, age, grad_conv, grad_conv_in, grad_mid_norm, grad_mid_b,
    grad_context, grad_context_n, grad_query, grad_key, grad_value, grad_norm_a,
    frames_out, mask_main, mask_rim, mask_next, stats, stats_n, delta, delta_n,
    early, early_x, early_y, early_z, early_all, late_sum, late_x, late_y, late_z,
    sums,
    send_sems, recv_sems, local_sems,
):
    dp, ctx = lax.axis_index("dp"), lax.axis_index("ctx")
    core = lax.rem(dp, 2)
    x = lax.rem(lax.div(dp, 2), NX)
    y_lo = lax.div(dp, 2 * NX)
    z = lax.div(ctx, NY // 2)
    y = lax.rem(ctx, NY // 2) * 2 + y_lo
    offset = ctx * ROWS
    group = x * 2 + core

    def at(px, py, pz, pc):
        return ((lax.rem(py, 2) * NX + px) * 2 + pc, pz * (NY // 2) + lax.div(py, 2))

    def shift(value, step, size):
        return lax.rem(value + (step + size), size)

    def frames_at(step):
        return (dp, shift(ctx, step, 4 * NZ))

    sibling = (dp + 1 - 2 * core, ctx)
    right, left = at(shift(x, 1, NX), y, z, core), at(shift(x, -1, NX), y, z, core)
    above, below = at(x, shift(y, 1, NY), z, core), at(x, shift(y, -1, NY), z, core)
    front, back = at(x, y, shift(z, 1, NZ), core), at(x, y, shift(z, -1, NZ), core)
    later, earlier, later_2 = frames_at(1), frames_at(-1), frames_at(2)

    def group_peer(step):
        other = shift(group, step, GROUP)
        return other, at(lax.div(other, 2), y, z, lax.rem(other, 2))

    def y_peer(step):
        other = shift(y, step, NY)
        return other, at(x, other, z, core)

    def z_peer(step):
        other = shift(z, step, NZ)
        return other, at(x, y, other, core)

    links = Links(send_sems, recv_sems)
    local = []

    def bring(source, target):
        copy = pltpu.make_async_copy(source, target, local_sems.at[len(local)])
        copy.start()
        local.append(copy)
        return copy

    own_rows = pl.ds(pl.multiple_of(dp * DEEP, DEEP), DEEP)
    got_weights = [
        bring(source, weights.at[index, own_rows, :])
        for index, source in ((0, w_key), (1, w_value), (2, w_query), (3, w_output))
    ]
    got_frames = bring(frames.at[0], xs.at[pl.ds(0, ROWS), :])
    got_rest = [
        bring(cotangent.at[0], cts.at[pl.ds(0, ROWS), :]),
        bring(att_gain, gain_a),
        bring(conv_gain, gain_c),
        bring(kernel, taps_ref),
        bring(bias, bias_ref),
    ]

    barrier = pltpu.get_barrier_semaphore()
    peers = [group_peer(step)[1] for step in range(1, GROUP)]
    peers += [y_peer(step)[1] for step in range(1, NY)]
    peers += [z_peer(step)[1] for step in range(1, NZ)]
    peers += [later, earlier, later_2, frames_at(-2)]
    for peer in peers:
        pl.semaphore_signal(barrier, inc=1, device_id=peer, device_id_type=MESH)
    for copy in got_weights:
        copy.wait()
    pl.semaphore_wait(barrier, len(peers))

    half = lax.rem(z, 2)

    def shard(index, of_core):
        if index is None:
            return (y_lo * NX + x) * 2 + of_core
        step, other = SHARDS[index]
        side = 1 - y_lo if other else y_lo
        return (side * NX + shift(x, step, NX)) * 2 + of_core

    def piece(index, of_half, part, wave, of_core):
        first, size = shard(index, of_core) * DEEP, DEEP
        if of_half is not None:
            first, size = first + of_half * 32, 32
        if part is not None:
            first, size = first + part * 16, 16
        return weights.at[pl.ds(2 * wave, 2), pl.ds(pl.multiple_of(first, 16), size), :]

    def give(name, index, of_half, part, wave, device):
        ref = piece(index, of_half, part, wave, core)
        links.send((name, wave), ref, ref, device)

    def take(name, index, of_half, part, wave, of_core=None):
        ref = piece(index, of_half, part, wave, core if of_core is None else of_core)
        links.arrived((name, wave), ref, sibling)

    siblings = []

    def pass_on(name, index, of_half, part, wave):
        give("sib" + name, index, of_half, part, wave, sibling)
        siblings.append((name, index, of_half, part, wave))

    def pass_z(index, parts, wave):
        for part in parts:
            give(f"z{part}{index}", index, half, part, wave, (front, back)[part])

    for wave in (0, 1):
        give("0", None, half, None, wave, right)
        give("1", None, half, None, wave, left)
        give("3", None, half, None, wave, below)
        pass_on("own", None, None, None, wave)

    links.send("prev", frames.at[0], xs.at[pl.ds(ROWS, ROWS), :], later)
    links.send("next", frames.at[0, pl.ds(0, RIM), :], xs.at[pl.ds(2 * ROWS + RIM, RIM), :], earlier)
    links.send("prev2", frames.at[0, pl.ds(ROWS - RIM, RIM), :], xs.at[pl.ds(2 * ROWS, RIM), :], later_2)
    links.send("cot", cotangent.at[0, pl.ds(0, RIM), :], cts.at[pl.ds(ROWS, RIM), :], earlier)

    got_frames.wait()
    for copy in got_rest:
        copy.wait()

    def norm_rows(first, size, own):
        block = xs[pl.ds(first, size), :].astype(F32)
        scaled, inverse = normalize(block)
        norm_b[pl.ds(first, size), :] = (scaled * gain_a[...]).astype(BF16)
        if own is not None:
            scaled_a[pl.ds(first, size), :] = scaled
        if own:
            inverse_a[pl.ds(first, size), :] = wide(inverse, 128)
            mid[pl.ds(pl.multiple_of(first + 8, 8), size), :] = block
        return block

    @pl.loop(0, 4)
    def _(step):
        norm_rows(pl.multiple_of(step * 32, 32), 32, True)

    ends = [jnp.int32(0)]
    for record in range(lengths.shape[1]):
        ends.append(ends[-1] + lengths[0, record])

    def start_of(places):
        start = jnp.full(places.shape, BEFORE, jnp.int32)
        for end in ends:
            start = jnp.where(places >= end, end, start)
        return start

    def mask_of(query_places, key_places):
        first = jnp.maximum(start_of(query_places), query_places - LEFT)
        return jnp.where((key_places <= query_places) & (key_places >= first), 0.0, FAR).astype(F32)

    square = (ROWS, ROWS)
    place_rows, place_lanes = offset + iota(square, 0), offset + iota(square, 1)
    mask_main[:, :ROWS] = mask_of(place_rows, place_lanes)
    mask_main[:, ROWS:] = mask_of(place_rows, place_lanes - ROWS)
    mask_next[...] = mask_of(place_lanes + ROWS, place_rows)
    rim_rows = iota((16, EXT), 0)
    rim_places = offset + jnp.where(rim_rows < 8, rim_rows - 8, rim_rows + (ROWS - 8))
    lanes = iota((16, EXT), 1)
    rim_keys = jnp.where(lanes < ROWS, lanes, lanes - 2 * ROWS)
    rim_keys = jnp.where(lanes < 2 * ROWS, rim_keys, lanes - (3 * ROWS + RIM))
    rim_keys = offset + jnp.where(lanes < 2 * ROWS + RIM, rim_keys, lanes - (ROWS + RIM))
    mask_rim[...] = mask_of(rim_places, rim_keys)
    age_rows = offset + iota((ROWS + 8, 128), 0)
    age[...] = age_rows - start_of(age_rows)

    for wave in (0, 1):
        take("0", 0, half, None, wave)
        give("20", 0, half, 0, wave, right)
        take("1", 1, half, None, wave)
        give("21", 1, half, 1, wave, left)
        take("3", 3, half, None, wave)
        give("4", 3, half, None, wave, right)
        give("5", 3, half, None, wave, left)
        for index in (0, 1, 3):
            pass_z(index, (0, 1), wave)
            pass_on(str(index), index, half, None, wave)
    for wave in (0, 1):
        take("4", 4, half, None, wave)
        give("60", 4, half, 0, wave, right)
        take("5", 5, half, None, wave)
        give("61", 5, half, 1, wave, left)
        for part in (0, 1):
            take(f"2{part}", 2, half, part, wave)
            pass_z(2, (part,), wave)
            pass_on(f"2{part}", 2, half, part, wave)
        for index in (4, 5):
            pass_z(index, (0, 1), wave)
            pass_on(str(index), index, half, None, wave)
    for wave in (0, 1):
        for part in (0, 1):
            take(f"6{part}", 6, half, part, wave)
            pass_z(6, (part,), wave)
            pass_on(f"6{part}", 6, half, part, wave)
        for index in (0, 1, 3, 2, 4, 5, 6):
            for part in (0, 1):
                take(f"z{part}{index}", index, 1 - half, part, wave)
                pass_on(f"z{part}{index}", index, 1 - half, part, wave)

    links.arrived("prev", xs.at[pl.ds(ROWS, ROWS), :], earlier)
    links.arrived("next", xs.at[pl.ds(2 * ROWS + RIM, RIM), :], earlier)
    links.arrived("prev2", xs.at[pl.ds(2 * ROWS, RIM), :], earlier)
    links.arrived("cot", cts.at[pl.ds(ROWS, RIM), :], earlier)

    @pl.loop(4, 8)
    def _(step):
        norm_rows(pl.multiple_of(step * 32, 32), 32, False)

    block = norm_rows(2 * ROWS, 2 * RIM, None)
    mid[pl.ds(ROWS + 8, 8), :] = block[RIM : RIM + 8]
    mid[pl.ds(0, 8), :] = xs[pl.ds(2 * ROWS - RIM, RIM), :].astype(F32)[8:]

    for name, index, of_half, part, wave in siblings:
        take("sib" + name, index, of_half, part, wave, 1 - core)

    normed = norm_b[...]
    keys[...] = dot(normed, weights[0]).astype(BF16)
    values[...] = dot(normed, weights[1]).astype(BF16)
    rows = jnp.concatenate(
        [normed[:ROWS], normed[2 * ROWS - RIM : 2 * ROWS], normed[2 * ROWS + RIM :]], axis=0
    )
    projected = dot(rows, weights[2])
    query[...] = projected[:ROWS].astype(BF16)
    query_e[...] = projected[ROWS + 8 : ROWS + 24].astype(BF16)
    links.send("query", query, query_n, earlier)

    def head(index):
        return slice(index * HEAD_DIM, (index + 1) * HEAD_DIM)

    lane = iota(square, 1)
    columns = jnp.zeros(square, F32)
    for h in range(HEADS):
        scores = dot_nt(query[:, head(h)], keys[: 2 * ROWS, head(h)]) * SCALE + mask_main[...]
        top = jnp.max(scores, axis=-1, keepdims=True)
        shifted = jnp.exp(scores - top)
        part = 1.0 / jnp.sum(shifted, axis=-1, keepdims=True)
        share = shifted * part
        probs[h] = share
        context[8 : ROWS + 8, head(h)] = dot(share.astype(BF16), values[: 2 * ROWS, head(h)])
        columns = jnp.where(lane == h, top, columns)
        columns = jnp.where(lane == HEADS + h, part, columns)
        scores = dot_nt(query_e[:, head(h)], keys[:, head(h)]) * SCALE + mask_rim[...]
        shifted = jnp.exp(scores - jnp.max(scores, axis=-1, keepdims=True))
        share = shifted * (1.0 / jnp.sum(shifted, axis=-1, keepdims=True))
        rims = dot(share.astype(BF16), values[:, head(h)])
        context[0:8, head(h)] = rims[:8]
        context[ROWS + 8 :, head(h)] = rims[8:]
    stats[...] = columns.T[:8]
    links.send("stats", stats, stats_n, earlier)

    mid[...] += dot_nt(context[...].astype(BF16), weights[3])

    @pl.loop(0, 3)
    def _(step):
        part_rows = pl.ds(pl.multiple_of(step * 48, 8), 48)
        scaled, inverse = normalize(mid[part_rows, :])
        scaled_c[part_rows, :] = scaled
        inverse_c[part_rows, :] = wide(inverse, 128)
        normed = (scaled * gain_c[...]).astype(BF16).astype(F32)
        for tile in range(WIDTH // 128):
            conv_in[tile, part_rows, :] = normed[:, tile * 128 : (tile + 1) * 128]

    @pl.loop(0, WIDTH // 128)
    def _(tile):
        part_lanes = pl.ds(pl.multiple_of(tile * 128, 128), 128)
        conv = jnp.broadcast_to(bias_ref[:, part_lanes], (ROWS + 8, 128))
        for back_by in range(TAPS):
            term = conv_in[tile, pl.ds(8 - back_by, ROWS + 8), :]
            term = term * taps_ref[TAPS - 1 - back_by : TAPS - back_by, part_lanes]
            conv = conv + jnp.where(age[...] >= back_by, term, 0.0)
        gate = 1.0 / (1.0 + jnp.exp(-conv))
        grad_out = cts[:, part_lanes].astype(F32)[: ROWS + 8]
        grad = grad_out * gate * (1.0 + conv * (1.0 - gate))
        grad_conv[...] = grad
        grad = grad[:ROWS]
        early[tile, 9:10, :] = jnp.sum(grad, axis=0, keepdims=True)
        total = jnp.zeros((ROWS, 128), F32)
        for back_by in range(TAPS):
            tap = TAPS - 1 - back_by
            kept = jnp.where(age[:ROWS, :] >= back_by, grad, 0.0)
            term = kept * conv_in[tile, pl.ds(8 - back_by, ROWS), :]
            early[tile, tap : tap + 1, :] = jnp.sum(term, axis=0, keepdims=True)
            ahead = pl.ds(back_by, ROWS)
            kept = jnp.where(age[ahead, :] >= back_by, grad_conv[ahead, :], 0.0)
            total = total + kept * taps_ref[tap : tap + 1, part_lanes]
        grad_conv_in[:, part_lanes] = total
        term = total * scaled_c[8 : ROWS + 8, part_lanes]
        early[tile, 10:11, :] = jnp.sum(term, axis=0, keepdims=True)
        early[tile, 11:16, :] = jnp.zeros((5, 128), F32)

    def collect(name, me, size, slots):
        for step in range(1, size):
            links.arrived((name, step), slots.at[shift(me, -step, size)], sibling)
        total = slots[0]
        for index in range(1, size):
            total = total + slots[index]
        return total

    early_x[group] = early[group]
    for step in range(1, GROUP):
        other, device = group_peer(step)
        links.send(("ex", step), early.at[other], early_x.at[group], device)

    @pl.loop(0, 4)
    def _(step):
        part_rows = pl.ds(pl.multiple_of(step * 32, 32), 32)
        ext_rows = pl.ds(pl.multiple_of(step * 32 + 8, 8), 32)
        grad, scaled = grad_conv_in[part_rows, :] * gain_c[...], scaled_c[ext_rows, :]
        first = jnp.mean(grad, axis=-1, keepdims=True)
        second = jnp.mean(grad * scaled, axis=-1, keepdims=True)
        result = spread(inverse_c[ext_rows, :]) * (grad - first - scaled * second)
        grad_mid_norm[part_rows, :] = result
        grad_mid_b[part_rows, :] = (cts[part_rows, :].astype(F32) + result).astype(BF16)

    grad_context[...] = dot(grad_mid_b[...], weights[3]).astype(BF16)
    links.send("grad", grad_context, grad_context_n, earlier)
    columns = jnp.zeros(square, F32)
    deltas = []
    for h in range(HEADS):
        term = context[8 : ROWS + 8, head(h)] * grad_context[:, head(h)].astype(F32)
        deltas.append(jnp.sum(term, axis=-1, keepdims=True))
        columns = jnp.where(lane == h, deltas[h], columns)
    delta[...] = columns.T[:8]
    links.send("delta", delta, delta_n, earlier)

    for h in range(HEADS):
        grad_h = grad_context[:, head(h)]
        share = probs[h]
        grad_probs = dot_nt(grad_h, values[: 2 * ROWS, head(h)])
        grad_scores = (share * (grad_probs - deltas[h]) * SCALE).astype(BF16)
        grad_query[:, head(h)] = dot(grad_scores, keys[: 2 * ROWS, head(h)]).astype(BF16)
        grad_key[:, head(h)] = dot_tn(grad_scores, query[:, head(h)]).astype(BF16)
        grad_value[:, head(h)] = dot_tn(share.astype(BF16), grad_h).astype(BF16)

    parts = dot_nt(grad_key[...], weights[0]) + dot_nt(grad_value[...], weights[1])
    own_part = parts[:ROWS] + dot_nt(grad_query[...], weights[2])
    grad_norm_a[...] = own_part
    product = own_part * scaled_a[:ROWS] + parts[ROWS:] * scaled_a[ROWS:]
    total = jnp.sum(product, axis=0, keepdims=True)
    for tile in range(WIDTH // 128):
        late_sum[tile : tile + 1, :] = total[:, tile * 128 : (tile + 1) * 128]
    late_x[group] = late_sum[...]
    for step in range(1, GROUP):
        links.send(("lx", step), late_x.at[group], late_x.at[group], group_peer(step)[1])

    early_y[y] = collect("ex", group, GROUP, early_x)
    for step in range(1, NY):
        links.send(("ey", step), early_y.at[y], early_y.at[y], y_peer(step)[1])
    late_y[y] = collect("lx", group, GROUP, late_x)
    for step in range(1, NY):
        links.send(("ly", step), late_y.at[y], late_y.at[y], y_peer(step)[1])
    early_z[z] = collect("ey", y, NY, early_y)
    for step in range(1, NZ):
        links.send(("ez", step), early_z.at[z], early_z.at[z], z_peer(step)[1])

    links.arrived("query", query_n, earlier)
    links.arrived("stats", stats_n, earlier)
    links.arrived("grad", grad_context_n, earlier)
    links.arrived("delta", delta_n, earlier)
    for h in range(HEADS):
        query_h, grad_h = query_n[:, head(h)], grad_context_n[:, head(h)]
        scores = dot_nt(keys[:ROWS, head(h)], query_h) * SCALE + mask_next[...]
        share = jnp.exp(scores - stats_n[h : h + 1, :]) * stats_n[HEADS + h : HEADS + h + 1, :]
        grad_probs = dot_nt(values[:ROWS, head(h)], grad_h)
        grad_scores = (share * (grad_probs - delta_n[h : h + 1, :]) * SCALE).astype(BF16)
        grad_key[:ROWS, head(h)] = dot(grad_scores, query_h).astype(BF16)
        grad_value[:ROWS, head(h)] = dot(share.astype(BF16), grad_h).astype(BF16)

    late_z[z] = collect("ly", y, NY, late_y)
    for step in range(1, NZ):
        links.send(("lz", step), late_z.at[z], late_z.at[z], z_peer(step)[1])
    early_all[group] = collect("ez", z, NZ, early_z)
    for step in range(1, GROUP):
        links.send(("ea", step), early_all.at[group], early_all.at[group], group_peer(step)[1])

    grad_norm_a[...] += dot_nt(grad_key[:ROWS], weights[0]) + dot_nt(grad_value[:ROWS], weights[1])

    @pl.loop(0, 4)
    def _(step):
        part_rows = pl.ds(pl.multiple_of(step * 32, 32), 32)
        grad, scaled = grad_norm_a[part_rows, :] * gain_a[...], scaled_a[part_rows, :]
        first = jnp.mean(grad, axis=-1, keepdims=True)
        second = jnp.mean(grad * scaled, axis=-1, keepdims=True)
        result = spread(inverse_a[part_rows, :]) * (grad - first - scaled * second)
        frames_out[part_rows, :] = grad_mid_norm[part_rows, :] + result

    out_copy = bring(frames_out, out_frames.at[0])
    links.finish()

    factor = 1.0 / math.sqrt(NX * 2 * 2 * (NY // 2) * NZ * ROWS)
    for step in range(1, GROUP):
        links.arrived(("ea", step), early_all.at[shift(group, -step, GROUP)], sibling)
    for tile in range(WIDTH // 128):
        sums[:, tile * 128 : (tile + 1) * 128] = early_all[tile] * factor
    summed = collect("lz", z, NZ, late_z) * factor
    for tile in range(WIDTH // 128):
        sums[11:12, tile * 128 : (tile + 1) * 128] = summed[tile : tile + 1]
    bring(sums, out_sums).wait()
    out_copy.wait()


def finish_kernel(frames_in, sums, out_frames, out_att, out_conv, out_kernel, out_bias):
    out_frames[...] = frames_in[...]

    @pl.when(pl.program_id(0) == 0)
    def _():
        out_kernel[...] = sums[:TAPS]
        out_bias[...] = sums[9:10]
        out_conv[...] = sums[10:11]
        out_att[...] = sums[11:12]


def scratch():
    def buffer(*shape, dtype=F32):
        return pltpu.VMEM(shape, dtype)

    return [
        buffer(EXT, WIDTH, dtype=BF16),
        buffer(CONV, WIDTH, dtype=BF16),
        buffer(4, WIDTH, HEADS_WIDTH, dtype=BF16),
        buffer(1, WIDTH),
        buffer(1, WIDTH),
        buffer(TAPS, WIDTH),
        buffer(1, WIDTH),
        buffer(EXT, WIDTH, dtype=BF16),
        buffer(2 * ROWS, WIDTH),
        buffer(ROWS, 128),
        buffer(EXT, HEADS_WIDTH, dtype=BF16),
        buffer(EXT, HEADS_WIDTH, dtype=BF16),
        buffer(ROWS, HEADS_WIDTH, dtype=BF16),
        buffer(16, HEADS_WIDTH, dtype=BF16),
        buffer(ROWS, HEADS_WIDTH, dtype=BF16),
        buffer(HEADS, ROWS, 2 * ROWS),
        buffer(CONV, HEADS_WIDTH),
        buffer(CONV, WIDTH),
        buffer(CONV, WIDTH),
        buffer(CONV, 128),
        buffer(WIDTH // 128, CONV, 128),
        buffer(ROWS + 8, 128, dtype=jnp.int32),
        buffer(ROWS + 8, 128),
        buffer(ROWS, WIDTH),
        buffer(ROWS, WIDTH),
        buffer(ROWS, WIDTH, dtype=BF16),
        buffer(ROWS, HEADS_WIDTH, dtype=BF16),
        buffer(ROWS, HEADS_WIDTH, dtype=BF16),
        buffer(ROWS, HEADS_WIDTH, dtype=BF16),
        buffer(2 * ROWS, HEADS_WIDTH, dtype=BF16),
        buffer(2 * ROWS, HEADS_WIDTH, dtype=BF16),
        buffer(ROWS, WIDTH),
        buffer(ROWS, WIDTH),
        buffer(ROWS, 2 * ROWS),
        buffer(16, EXT),
        buffer(ROWS, ROWS),
        buffer(8, 128),
        buffer(8, 128),
        buffer(8, 128),
        buffer(8, 128),
        buffer(GROUP, 16, 128),
        buffer(GROUP, 16, 128),
        buffer(NY, 16, 128),
        buffer(NZ, 16, 128),
        buffer(GROUP, 16, 128),
        buffer(8, 128),
        buffer(GROUP, 8, 128),
        buffer(NY, 8, 128),
        buffer(NZ, 8, 128),
        buffer(16, WIDTH),
        pltpu.SemaphoreType.DMA((SLOTS,)),
        pltpu.SemaphoreType.DMA((SLOTS,)),
        pltpu.SemaphoreType.DMA((16,)),
    ]


def shards(
    frames, cotangent, lengths, w_query, w_key, w_value, w_output, att_gain, conv_gain, kernel, conv_bias
):
    row = (1, WIDTH)
    anywhere = pl.BlockSpec(memory_space=pl.ANY)
    in_specs = [anywhere] * 11
    in_specs[2] = pl.BlockSpec(memory_space=pltpu.SMEM)
    frames_sum, sums = pl.pallas_call(
        block_kernel,
        out_shape=(
            jax.ShapeDtypeStruct(frames.shape, F32),
            jax.ShapeDtypeStruct((16, WIDTH), F32),
        ),
        in_specs=in_specs,
        out_specs=(anywhere,) * 2,
        scratch_shapes=scratch(),
        compiler_params=pltpu.CompilerParams(
            collective_id=0, has_side_effects=True, vmem_limit_bytes=63 << 20
        ),
        cost_estimate=pl.CostEstimate(
            flops=3 << 30, bytes_accessed=4 << 20, transcendentals=1 << 20
        ),
    )(
        frames, cotangent, lengths, w_query, w_key, w_value, w_output.T,
        att_gain.reshape(row), conv_gain.reshape(row), kernel, conv_bias.reshape(row),
    )
    steps = 2
    moving = pl.BlockSpec((1, ROWS // steps, WIDTH), lambda step: (0, step, 0))

    def fixed(rows):
        return pl.BlockSpec((rows, WIDTH), lambda step: (0, 0))

    grad_frames, grad_att, grad_conv, grad_kernel, grad_bias = pl.pallas_call(
        finish_kernel,
        grid=(steps,),
        out_shape=(
            jax.ShapeDtypeStruct(frames.shape, F32),
            jax.ShapeDtypeStruct(row, F32),
            jax.ShapeDtypeStruct(row, F32),
            jax.ShapeDtypeStruct(kernel.shape, F32),
            jax.ShapeDtypeStruct(row, F32),
        ),
        in_specs=[moving, fixed(16)],
        out_specs=(moving, fixed(1), fixed(1), fixed(TAPS), fixed(1)),
        compiler_params=pltpu.CompilerParams(vmem_limit_bytes=63 << 20),
    )(frames_sum, sums)
    return (
        grad_frames,
        grad_att.reshape(WIDTH),
        grad_conv.reshape(WIDTH),
        grad_kernel,
        grad_bias.reshape(WIDTH),
    )


def solution(mesh):
    return jax.shard_map(
        shards,
        mesh=mesh,
        in_specs=(
            P("dp", "ctx", None),
            P("dp", "ctx", None),
            P("dp", None),
            P("dp", None),
            P("dp", None),
            P("dp", None),
            P(None, "dp"),
            P(),
            P(),
            P(),
            P(),
        ),
        out_specs=(P("dp", "ctx", None), P(), P(), P(), P()),
        check_vma=False,
    )
```

```python
import math

import jax
import jax.numpy as jnp
from jax import lax
from jax.experimental import pallas as pl
from jax.experimental.pallas import tpu as pltpu
from jax.sharding import PartitionSpec as P

MESH = pl.DeviceIdType.MESH
NX, NY, NZ = 4, 8, 8
ROWS = 128
WIDTH = 1024
HEADS = 4
HEAD_DIM = 128
HEADS_WIDTH = HEADS * HEAD_DIM
LEFT = 128
TAPS = 9
RIM = 16
EXT = 2 * ROWS + 2 * RIM
CONV = ROWS + 16
DEEP = 64
GROUP = 8
EPSILON = 1e-05
FAR = -1e30
BEFORE = -(1 << 20)
SCALE = HEAD_DIM ** (-0.5)
SLOTS = 176
F32 = jnp.float32
BF16 = jnp.bfloat16

SHARDS = ((-1, 0), (1, 0), (2, 0), (0, 1), (-1, 1), (1, 1), (2, 1), (0, 0))
DIRECT_SHARDS, FAR_SHARDS, OWN = (4, 5, 0, 1), (6, 2), 7
LATER, HALVED, FORWARD = (0, 1, 3), (4, 5, 6, 2), ((4, 0), (5, 0), (6, 0))
RELAYED = {0: (2, 0), 1: (2, 1), 4: (6, 0), 5: (6, 1)}


class Links:
    def __init__(self, send_sems, recv_sems):
        self.send_sems, self.recv_sems = send_sems, recv_sems
        self.names, self.sent = {}, []

    def copy(self, name, source, target, device):
        slot = self.names.setdefault(name, len(self.names))
        assert slot < SLOTS
        return pltpu.make_async_remote_copy(
            src_ref=source,
            dst_ref=target,
            send_sem=self.send_sems.at[slot],
            recv_sem=self.recv_sems.at[slot],
            device_id=device,
            device_id_type=MESH,
        )

    def send(self, name, source, target, device):
        copy = self.copy(name, source, target, device)
        copy.start()
        self.sent.append(copy)

    def arrived(self, name, target, device):
        self.copy(name, target, target, device).wait_recv()

    def finish(self):
        for copy in self.sent:
            copy.wait_send()


def dot(left, right):
    return jnp.dot(left, right, preferred_element_type=F32)


def dot_nt(left, right):
    return lax.dot_general(left, right, (((1,), (1,)), ((), ())), preferred_element_type=F32)


def dot_tn(left, right):
    return lax.dot_general(left, right, (((0,), (0,)), ((), ())), preferred_element_type=F32)


def normalize(values):
    center = values - jnp.mean(values, axis=-1, keepdims=True)
    inverse = lax.rsqrt(jnp.mean(center * center, axis=-1, keepdims=True) + EPSILON)
    return center * inverse, inverse


def wide(column, width):
    return jnp.broadcast_to(column, (column.shape[0], width))


def spread(block):
    return jnp.concatenate([block] * (WIDTH // 128), axis=1)


def iota(shape, axis):
    return lax.broadcasted_iota(jnp.int32, shape, axis)


def block_kernel(
    frames, cotangent, lengths, w_query, w_key, w_value, w_output, att_gain, conv_gain, kernel, bias,
    out_frames, out_sums,
    xs, cts, weights, gain_a, gain_c, taps_ref, bias_ref,
    norm_b, scaled_a, inverse_a, keys, values, query, query_e, query_n, probs, probs_rim, context, mid,
    scaled_c, inverse_c, conv_in, age, grad_conv, grad_conv_in, grad_mid_norm, grad_mid_b,
    grad_context, grad_context_n, grad_query, grad_key, grad_value, grad_norm_a,
    frames_out, mask_main, mask_rim, mask_next, stats, stats_n, delta, delta_n,
    early, early_x, early_y, early_z, early_all, late_sum, late_x, late_y, late_z,
    sums,
    send_sems, recv_sems, local_sems,
):
    dp, ctx = lax.axis_index("dp"), lax.axis_index("ctx")
    pair = lax.div(dp, 2)
    core = dp - 2 * pair
    y_lo = lax.div(pair, NX)
    x = pair - NX * y_lo
    z = lax.div(ctx, NY // 2)
    y_hi = ctx - (NY // 2) * z
    y = 2 * y_hi + y_lo
    offset = ctx * ROWS
    group = x * 2 + core

    def wrap(value, step, size):
        moved = value + step
        if isinstance(step, int) and step < 0:
            return jnp.where(moved < 0, moved + size, moved)
        return jnp.where(moved >= size, moved - size, moved)

    def flip(bit, change):
        return 1 - bit if change else bit

    def at(px, p_hi, p_lo, pz, pc):
        return ((p_lo * NX + px) * 2 + pc, pz * (NY // 2) + p_hi)

    def frames_at(step):
        return (dp, wrap(ctx, step, NZ * NY // 2))

    sibling = at(x, y_hi, y_lo, z, 1 - core)
    y_below = jnp.where(y_hi + y_lo == 0, NY // 2 - 1, y_hi + y_lo - 1)
    right, left = at(wrap(x, 1, NX), y_hi, y_lo, z, core), at(wrap(x, -1, NX), y_hi, y_lo, z, core)
    y_above = wrap(y_hi, y_lo, NY // 2)
    corners_above = [at(wrap(x, step, NX), y_above, 1 - y_lo, z, core) for step in (-1, 1)]
    corners_below = [at(wrap(x, step, NX), y_below, 1 - y_lo, z, core) for step in (-1, 1)]
    below = at(x, y_below, 1 - y_lo, z, core)
    front, back = at(x, y_hi, y_lo, wrap(z, 1, NZ), core), at(x, y_hi, y_lo, wrap(z, -1, NZ), core)
    later, earlier, later_2 = frames_at(1), frames_at(-1), frames_at(2)

    group_steps, y_steps, z_steps = [], [], []
    for step in (2, 1, -1, 0):
        for change in (1, 0):
            if (step, change) != (0, 0):
                to, of = wrap(x, step, NX), wrap(x, -step, NX)
                pc = flip(core, change)
                group_steps.append(((step, change), to * 2 + pc, at(to, y_hi, y_lo, z, pc), of * 2 + pc))
    for step in (2, -1, 1, 0):
        for change in (1, 0):
            if (step, change) != (0, 0):
                to, of = wrap(y_hi, step, NY // 2), wrap(y_hi, -step, NY // 2)
                lo = flip(y_lo, change)
                y_steps.append(((step, change), to * 2 + lo, at(x, to, lo, z, core), of * 2 + lo))
    for step in (4, 3, -3, 2, -2, 1, -1):
        to, of = wrap(z, step, NZ), wrap(z, -step, NZ)
        z_steps.append((step, to, at(x, y_hi, y_lo, to, core), of))

    links = Links(send_sems, recv_sems)
    local = []

    def bring(source, target):
        copy = pltpu.make_async_copy(source, target, local_sems.at[len(local)])
        copy.start()
        local.append(copy)
        return copy

    barrier = pltpu.get_barrier_semaphore()
    peers = [step[2] for step in group_steps + y_steps + z_steps]
    peers += [later, earlier, later_2, frames_at(-2)]
    peers += corners_above + corners_below
    for peer in peers:
        pl.semaphore_signal(barrier, inc=1, device_id=peer, device_id_type=MESH)

    own_rows = pl.ds(pl.multiple_of(dp * DEEP, DEEP), DEEP)
    got_weights = [
        bring(source, weights.at[index, own_rows, :])
        for index, source in ((0, w_key), (1, w_query), (2, w_value), (3, w_output))
    ]
    got_frames = bring(frames.at[0], xs.at[pl.ds(0, ROWS), :])
    got_rest = [
        bring(cotangent.at[0], cts.at[pl.ds(0, ROWS), :]),
        bring(att_gain, gain_a),
        bring(conv_gain, gain_c),
        bring(kernel, taps_ref),
        bring(bias, bias_ref),
    ]

    for copy in got_weights:
        copy.wait()
    pl.semaphore_wait(barrier, len(peers))

    half = z - 2 * lax.div(z, 2)

    def shard(index, of_core):
        step, other = SHARDS[index]
        return (flip(y_lo, other) * NX + wrap(x, step, NX)) * 2 + of_core

    def piece(index, of_half, part, wave, of_core):
        first, size = shard(index, of_core) * DEEP, DEEP
        if of_half is not None:
            first, size = first + of_half * 32, 32
        if part is not None:
            first, size = first + part * 16, 16
        return weights.at[pl.ds(2 * wave, 2), pl.ds(pl.multiple_of(first, 16), size), :]

    def give(name, index, of_half, part, wave, device):
        ref = piece(index, of_half, part, wave, core)
        links.send((name, wave), ref, ref, device)

    def take(name, index, of_half, part, wave, of_core=None):
        ref = piece(index, of_half, part, wave, core if of_core is None else of_core)
        links.arrived((name, wave), ref, sibling)

    siblings = []

    def pass_on(name, index, of_half, part, wave):
        give("sib" + name, index, of_half, part, wave, sibling)
        siblings.append((name, index, of_half, part, wave))

    targets = {0: right, 1: left, 3: below, 4: corners_below[1], 5: corners_below[0]}

    def give_own(wave):
        for index in DIRECT_SHARDS:
            ref = piece(OWN, half, None, wave, core)
            links.send((str(index), wave), ref, ref, targets[index])
        pass_on("own", OWN, None, None, wave)

    give_own(0)

    links.send("prev", frames.at[0], xs.at[pl.ds(ROWS, ROWS), :], later)
    links.send("next", frames.at[0, pl.ds(0, RIM), :], xs.at[pl.ds(2 * ROWS + RIM, RIM), :], earlier)
    links.send("prev2", frames.at[0, pl.ds(ROWS - RIM, RIM), :], xs.at[pl.ds(2 * ROWS, RIM), :], later_2)
    links.send("cot", cotangent.at[0, pl.ds(0, RIM), :], cts.at[pl.ds(ROWS, RIM), :], earlier)

    got_frames.wait()
    for copy in got_rest:
        copy.wait()

    def norm_rows(first, size, own):
        block = xs[pl.ds(first, size), :].astype(F32)
        scaled, inverse = normalize(block)
        norm_b[pl.ds(first, size), :] = (scaled * gain_a[...]).astype(BF16)
        if own is not None:
            scaled_a[pl.ds(first, size), :] = scaled
        if own:
            inverse_a[pl.ds(first, size), :] = wide(inverse, 128)
            mid[pl.ds(pl.multiple_of(first + 8, 8), size), :] = block
        return block

    @pl.loop(0, 4, unroll=True)
    def _(step):
        norm_rows(pl.multiple_of(step * 32, 32), 32, True)

    ends = [jnp.int32(0)]
    for record in range(lengths.shape[1]):
        ends.append(ends[-1] + lengths[0, record])

    def start_of(places):
        start = jnp.full(places.shape, BEFORE, jnp.int32)
        for end in ends:
            start = jnp.where(places >= end, end, start)
        return start

    def mask_of(query_places, key_places):
        first = jnp.maximum(start_of(query_places), query_places - LEFT)
        return jnp.where((key_places <= query_places) & (key_places >= first), 0.0, FAR).astype(F32)

    square = (ROWS, ROWS)
    place_rows, place_lanes = offset + iota(square, 0), offset + iota(square, 1)
    mask_main[:, :ROWS] = mask_of(place_rows, place_lanes)
    mask_main[:, ROWS:] = mask_of(place_rows, place_lanes - ROWS)
    mask_next[...] = mask_of(place_lanes + ROWS, place_rows)
    rim_rows = iota((16, EXT), 0)
    rim_places = offset + jnp.where(rim_rows < 8, rim_rows - 8, rim_rows + (ROWS - 8))
    lanes = iota((16, EXT), 1)
    rim_keys = jnp.where(lanes < ROWS, lanes, lanes - 2 * ROWS)
    rim_keys = jnp.where(lanes < 2 * ROWS, rim_keys, lanes - (3 * ROWS + RIM))
    rim_keys = offset + jnp.where(lanes < 2 * ROWS + RIM, rim_keys, lanes - (ROWS + RIM))
    mask_rim[...] = mask_of(rim_places, rim_keys)
    age_rows = offset + iota((ROWS + 8, 128), 0)
    age[...] = age_rows - start_of(age_rows)

    give_own(1)

    def pass_z(index, part, wave):
        give(f"z{part}{index}", index, half, part, wave, front if (index, part) in FORWARD else back)

    for wave in (0, 1):
        for index in DIRECT_SHARDS:
            take(str(index), index, half, None, wave)
            if index in RELAYED:
                further, part = RELAYED[index]
                give(f"{further}{part}", index, half, part, wave, (right, left)[part])
            if index in HALVED:
                for part in (0, 1):
                    pass_z(index, part, wave)
            pass_on(str(index), index, half, None, wave)
        for index in LATER:
            of_half = None if index == 3 else 1 - half
            ref = piece(OWN, of_half, None, wave, core)
            links.send((f"o{index}", wave), ref, ref, targets[index])
    for wave in (0, 1):
        for index in FAR_SHARDS:
            for part in (0, 1):
                take(f"{index}{part}", index, half, part, wave)
                pass_z(index, part, wave)
                pass_on(f"{index}{part}", index, half, part, wave)

    def take_rest(wave):
        for index in LATER:
            of_half = None if index == 3 else 1 - half
            take(f"o{index}", index, of_half, None, wave)
            pass_on(f"o{index}", index, of_half, None, wave)
        for index in HALVED:
            for part in (0, 1):
                take(f"z{part}{index}", index, 1 - half, part, wave)
                pass_on(f"z{part}{index}", index, 1 - half, part, wave)

    def take_siblings(of_wave):
        for name, index, of_half, part, wave in siblings:
            if wave == of_wave:
                take("sib" + name, index, of_half, part, wave, 1 - core)

    links.arrived("prev", xs.at[pl.ds(ROWS, ROWS), :], earlier)
    links.arrived("next", xs.at[pl.ds(2 * ROWS + RIM, RIM), :], earlier)
    links.arrived("prev2", xs.at[pl.ds(2 * ROWS, RIM), :], earlier)
    links.arrived("cot", cts.at[pl.ds(ROWS, RIM), :], earlier)

    @pl.loop(4, 8, unroll=True)
    def _(step):
        norm_rows(pl.multiple_of(step * 32, 32), 32, False)

    block = norm_rows(2 * ROWS, 2 * RIM, None)
    mid[pl.ds(ROWS + 8, 8), :] = block[RIM : RIM + 8]
    mid[pl.ds(0, 8), :] = xs[pl.ds(2 * ROWS - RIM, RIM), :].astype(F32)[8:]

    take_rest(0)
    take_siblings(0)

    normed = norm_b[...]
    keys[...] = dot(normed, weights[0]).astype(BF16)
    rows = jnp.concatenate(
        [normed[:ROWS], normed[2 * ROWS - RIM : 2 * ROWS], normed[2 * ROWS + RIM :]], axis=0
    )
    projected = dot(rows, weights[1])
    query[...] = projected[:ROWS].astype(BF16)
    query_e[...] = projected[ROWS + 8 : ROWS + 24].astype(BF16)
    links.send("query", query, query_n, earlier)
    take_rest(1)

    def head(index):
        return slice(index * HEAD_DIM, (index + 1) * HEAD_DIM)

    lane = iota(square, 1)
    columns = jnp.zeros(square, F32)
    for h in range(HEADS):
        scores = dot_nt(query[:, head(h)], keys[: 2 * ROWS, head(h)]) * SCALE + mask_main[...]
        top = jnp.max(scores, axis=-1, keepdims=True)
        shifted = jnp.exp(scores - top)
        part = 1.0 / jnp.sum(shifted, axis=-1, keepdims=True)
        probs[h] = shifted * part
        columns = jnp.where(lane == h, top, columns)
        columns = jnp.where(lane == HEADS + h, part, columns)
        scores = dot_nt(query_e[:, head(h)], keys[:, head(h)]) * SCALE + mask_rim[...]
        shifted = jnp.exp(scores - jnp.max(scores, axis=-1, keepdims=True))
        share = shifted * (1.0 / jnp.sum(shifted, axis=-1, keepdims=True))
        probs_rim[h] = share.astype(BF16)
    take_siblings(1)
    values[...] = dot(norm_b[...], weights[2]).astype(BF16)
    for h in range(HEADS):
        context[8 : ROWS + 8, head(h)] = dot(probs[h].astype(BF16), values[: 2 * ROWS, head(h)])
        rims = dot(probs_rim[h], values[:, head(h)])
        context[0:8, head(h)] = rims[:8]
        context[ROWS + 8 :, head(h)] = rims[8:]
    stats[...] = columns.T[:8]
    links.send("stats", stats, stats_n, earlier)

    mid[...] += dot_nt(context[...].astype(BF16), weights[3])

    @pl.loop(0, 3, unroll=True)
    def _(step):
        part_rows = pl.ds(pl.multiple_of(step * 48, 8), 48)
        scaled, inverse = normalize(mid[part_rows, :])
        scaled_c[part_rows, :] = scaled
        inverse_c[part_rows, :] = wide(inverse, 128)
        normed = (scaled * gain_c[...]).astype(BF16).astype(F32)
        for tile in range(WIDTH // 128):
            conv_in[tile, part_rows, :] = normed[:, tile * 128 : (tile + 1) * 128]

    @pl.loop(0, WIDTH // 128)
    def _(tile):
        part_lanes = pl.ds(pl.multiple_of(tile * 128, 128), 128)
        conv = jnp.broadcast_to(bias_ref[:, part_lanes], (ROWS + 8, 128))
        for back_by in range(TAPS):
            term = conv_in[tile, pl.ds(8 - back_by, ROWS + 8), :]
            term = term * taps_ref[TAPS - 1 - back_by : TAPS - back_by, part_lanes]
            conv = conv + jnp.where(age[...] >= back_by, term, 0.0)
        gate = 1.0 / (1.0 + jnp.exp(-conv))
        grad_out = cts[:, part_lanes].astype(F32)[: ROWS + 8]
        grad = grad_out * gate * (1.0 + conv * (1.0 - gate))
        grad_conv[...] = grad
        grad = grad[:ROWS]
        early[tile, 9:10, :] = jnp.sum(grad, axis=0, keepdims=True)
        total = jnp.zeros((ROWS, 128), F32)
        for back_by in range(TAPS):
            tap = TAPS - 1 - back_by
            kept = jnp.where(age[:ROWS, :] >= back_by, grad, 0.0)
            term = kept * conv_in[tile, pl.ds(8 - back_by, ROWS), :]
            early[tile, tap : tap + 1, :] = jnp.sum(term, axis=0, keepdims=True)
            ahead = pl.ds(back_by, ROWS)
            kept = jnp.where(age[ahead, :] >= back_by, grad_conv[ahead, :], 0.0)
            total = total + kept * taps_ref[tap : tap + 1, part_lanes]
        grad_conv_in[:, part_lanes] = total
        term = total * scaled_c[8 : ROWS + 8, part_lanes]
        early[tile, 10:11, :] = jnp.sum(term, axis=0, keepdims=True)
        early[tile, 11:16, :] = jnp.zeros((5, 128), F32)

    def spread_out(name, slots, me, steps):
        for step, _, device, _ in steps:
            links.send((name, step), slots.at[me], slots.at[me], device)

    def collect(name, slots, steps):
        for step, _, _, source in steps:
            links.arrived((name, step), slots.at[source], sibling)
        total = slots[0]
        for index in range(1, slots.shape[0]):
            total = total + slots[index]
        return total

    early_x[group] = early[group]
    for step, other, device, _ in group_steps:
        links.send(("ex", step), early.at[other], early_x.at[group], device)

    @pl.loop(0, 4, unroll=True)
    def _(step):
        part_rows = pl.ds(pl.multiple_of(step * 32, 32), 32)
        ext_rows = pl.ds(pl.multiple_of(step * 32 + 8, 8), 32)
        grad, scaled = grad_conv_in[part_rows, :] * gain_c[...], scaled_c[ext_rows, :]
        first = jnp.mean(grad, axis=-1, keepdims=True)
        second = jnp.mean(grad * scaled, axis=-1, keepdims=True)
        result = spread(inverse_c[ext_rows, :]) * (grad - first - scaled * second)
        grad_mid_norm[part_rows, :] = result
        grad_mid_b[part_rows, :] = (cts[part_rows, :].astype(F32) + result).astype(BF16)

    grad_context[...] = dot(grad_mid_b[...], weights[3]).astype(BF16)
    links.send("grad", grad_context, grad_context_n, earlier)
    deltas = []
    for h in range(HEADS):
        term = context[8 : ROWS + 8, head(h)] * grad_context[:, head(h)].astype(F32)
        deltas.append(jnp.sum(term, axis=-1, keepdims=True))

    for h in range(HEADS):
        grad_h = grad_context[:, head(h)]
        share = probs[h]
        grad_probs = dot_nt(grad_h, values[: 2 * ROWS, head(h)])
        grad_scores = (share * (grad_probs - deltas[h]) * SCALE).astype(BF16)
        grad_query[:, head(h)] = dot(grad_scores, keys[: 2 * ROWS, head(h)]).astype(BF16)
        grad_key[:, head(h)] = dot_tn(grad_scores, query[:, head(h)]).astype(BF16)
        grad_value[:, head(h)] = dot_tn(share.astype(BF16), grad_h).astype(BF16)

    parts = dot_nt(grad_key[...], weights[0]) + dot_nt(grad_value[...], weights[2])
    own_part = parts[:ROWS] + dot_nt(grad_query[...], weights[1])
    grad_norm_a[...] = own_part
    product = own_part * scaled_a[:ROWS] + parts[ROWS:] * scaled_a[ROWS:]
    total = jnp.sum(product, axis=0, keepdims=True)
    for tile in range(WIDTH // 128):
        late_sum[tile : tile + 1, :] = total[:, tile * 128 : (tile + 1) * 128]
    late_x[group] = late_sum[...]
    spread_out("lx", late_x, group, group_steps)

    columns = jnp.zeros(square, F32)
    for h in range(HEADS):
        columns = jnp.where(lane == h, deltas[h], columns)
    delta[...] = columns.T[:8]
    links.send("delta", delta, delta_n, earlier)

    early_z[z] = collect("ex", early_x, group_steps)
    spread_out("ez", early_z, z, z_steps)
    late_z[z] = collect("lx", late_x, group_steps)
    spread_out("lz", late_z, z, z_steps)
    early_y[y] = collect("ez", early_z, z_steps)
    spread_out("ey", early_y, y, y_steps)

    links.arrived("query", query_n, earlier)
    links.arrived("stats", stats_n, earlier)
    links.arrived("grad", grad_context_n, earlier)
    links.arrived("delta", delta_n, earlier)
    for h in range(HEADS):
        query_h, grad_h = query_n[:, head(h)], grad_context_n[:, head(h)]
        scores = dot_nt(keys[:ROWS, head(h)], query_h) * SCALE + mask_next[...]
        share = jnp.exp(scores - stats_n[h : h + 1, :]) * stats_n[HEADS + h : HEADS + h + 1, :]
        grad_probs = dot_nt(values[:ROWS, head(h)], grad_h)
        grad_scores = (share * (grad_probs - delta_n[h : h + 1, :]) * SCALE).astype(BF16)
        grad_key[:ROWS, head(h)] = dot(grad_scores, query_h).astype(BF16)
        grad_value[:ROWS, head(h)] = dot(share.astype(BF16), grad_h).astype(BF16)

    late_y[y] = collect("lz", late_z, z_steps)
    spread_out("ly", late_y, y, y_steps)
    early_all[group] = collect("ey", early_y, y_steps)
    spread_out("ea", early_all, group, group_steps)

    grad_norm_a[...] += dot_nt(grad_key[:ROWS], weights[0]) + dot_nt(grad_value[:ROWS], weights[2])

    @pl.loop(0, 4, unroll=True)
    def _(step):
        part_rows = pl.ds(pl.multiple_of(step * 32, 32), 32)
        grad, scaled = grad_norm_a[part_rows, :] * gain_a[...], scaled_a[part_rows, :]
        first = jnp.mean(grad, axis=-1, keepdims=True)
        second = jnp.mean(grad * scaled, axis=-1, keepdims=True)
        result = spread(inverse_a[part_rows, :]) * (grad - first - scaled * second)
        frames_out[part_rows, :] = grad_mid_norm[part_rows, :] + result

    out_copy = bring(frames_out, out_frames.at[0])
    links.finish()

    factor = 1.0 / math.sqrt(NX * 2 * 2 * (NY // 2) * NZ * ROWS)
    for step, _, _, source in group_steps:
        links.arrived(("ea", step), early_all.at[source], sibling)
    for tile in range(WIDTH // 128):
        sums[:, tile * 128 : (tile + 1) * 128] = early_all[tile] * factor
    summed = collect("ly", late_y, y_steps) * factor
    for tile in range(WIDTH // 128):
        sums[11:12, tile * 128 : (tile + 1) * 128] = summed[tile : tile + 1]
    bring(sums, out_sums).wait()
    out_copy.wait()


def finish_kernel(frames_in, sums, out_frames, out_att, out_conv, out_kernel, out_bias):
    out_frames[...] = frames_in[...]

    @pl.when(pl.program_id(0) == 0)
    def _():
        out_kernel[...] = sums[:TAPS]
        out_bias[...] = sums[9:10]
        out_conv[...] = sums[10:11]
        out_att[...] = sums[11:12]


def scratch():
    def buffer(*shape, dtype=F32):
        return pltpu.VMEM(shape, dtype)

    return [
        buffer(EXT, WIDTH, dtype=BF16),
        buffer(CONV, WIDTH, dtype=BF16),
        buffer(4, WIDTH, HEADS_WIDTH, dtype=BF16),
        buffer(1, WIDTH),
        buffer(1, WIDTH),
        buffer(TAPS, WIDTH),
        buffer(1, WIDTH),
        buffer(EXT, WIDTH, dtype=BF16),
        buffer(2 * ROWS, WIDTH),
        buffer(ROWS, 128),
        buffer(EXT, HEADS_WIDTH, dtype=BF16),
        buffer(EXT, HEADS_WIDTH, dtype=BF16),
        buffer(ROWS, HEADS_WIDTH, dtype=BF16),
        buffer(16, HEADS_WIDTH, dtype=BF16),
        buffer(ROWS, HEADS_WIDTH, dtype=BF16),
        buffer(HEADS, ROWS, 2 * ROWS),
        buffer(HEADS, 16, EXT, dtype=BF16),
        buffer(CONV, HEADS_WIDTH),
        buffer(CONV, WIDTH),
        buffer(CONV, WIDTH),
        buffer(CONV, 128),
        buffer(WIDTH // 128, CONV, 128),
        buffer(ROWS + 8, 128, dtype=jnp.int32),
        buffer(ROWS + 8, 128),
        buffer(ROWS, WIDTH),
        buffer(ROWS, WIDTH),
        buffer(ROWS, WIDTH, dtype=BF16),
        buffer(ROWS, HEADS_WIDTH, dtype=BF16),
        buffer(ROWS, HEADS_WIDTH, dtype=BF16),
        buffer(ROWS, HEADS_WIDTH, dtype=BF16),
        buffer(2 * ROWS, HEADS_WIDTH, dtype=BF16),
        buffer(2 * ROWS, HEADS_WIDTH, dtype=BF16),
        buffer(ROWS, WIDTH),
        buffer(ROWS, WIDTH),
        buffer(ROWS, 2 * ROWS),
        buffer(16, EXT),
        buffer(ROWS, ROWS),
        buffer(8, 128),
        buffer(8, 128),
        buffer(8, 128),
        buffer(8, 128),
        buffer(GROUP, 16, 128),
        buffer(GROUP, 16, 128),
        buffer(NY, 16, 128),
        buffer(NZ, 16, 128),
        buffer(GROUP, 16, 128),
        buffer(8, 128),
        buffer(GROUP, 8, 128),
        buffer(NY, 8, 128),
        buffer(NZ, 8, 128),
        buffer(16, WIDTH),
        pltpu.SemaphoreType.DMA((SLOTS,)),
        pltpu.SemaphoreType.DMA((SLOTS,)),
        pltpu.SemaphoreType.DMA((16,)),
    ]


def shards(
    frames, cotangent, lengths, w_query, w_key, w_value, w_output, att_gain, conv_gain, kernel, conv_bias
):
    row = (1, WIDTH)
    anywhere = pl.BlockSpec(memory_space=pl.ANY)
    in_specs = [anywhere] * 11
    in_specs[2] = pl.BlockSpec(memory_space=pltpu.SMEM)
    frames_sum, sums = pl.pallas_call(
        block_kernel,
        out_shape=(
            jax.ShapeDtypeStruct(frames.shape, F32),
            jax.ShapeDtypeStruct((16, WIDTH), F32),
        ),
        in_specs=in_specs,
        out_specs=(anywhere,) * 2,
        scratch_shapes=scratch(),
        compiler_params=pltpu.CompilerParams(
            collective_id=0, has_side_effects=True, vmem_limit_bytes=63 << 20
        ),
        cost_estimate=pl.CostEstimate(
            flops=3 << 30, bytes_accessed=4 << 20, transcendentals=1 << 20
        ),
    )(
        frames, cotangent, lengths, w_query, w_key, w_value, w_output.T,
        att_gain.reshape(row), conv_gain.reshape(row), kernel, conv_bias.reshape(row),
    )
    steps = 2
    moving = pl.BlockSpec((1, ROWS // steps, WIDTH), lambda step: (0, step, 0))

    def fixed(rows):
        return pl.BlockSpec((rows, WIDTH), lambda step: (0, 0))

    grad_frames, grad_att, grad_conv, grad_kernel, grad_bias = pl.pallas_call(
        finish_kernel,
        grid=(steps,),
        out_shape=(
            jax.ShapeDtypeStruct(frames.shape, F32),
            jax.ShapeDtypeStruct(row, F32),
            jax.ShapeDtypeStruct(row, F32),
            jax.ShapeDtypeStruct(kernel.shape, F32),
            jax.ShapeDtypeStruct(row, F32),
        ),
        in_specs=[moving, fixed(16)],
        out_specs=(moving, fixed(1), fixed(1), fixed(TAPS), fixed(1)),
        compiler_params=pltpu.CompilerParams(vmem_limit_bytes=63 << 20),
    )(frames_sum, sums)
    return (
        grad_frames,
        grad_att.reshape(WIDTH),
        grad_conv.reshape(WIDTH),
        grad_kernel,
        grad_bias.reshape(WIDTH),
    )


def solution(mesh):
    return jax.shard_map(
        shards,
        mesh=mesh,
        in_specs=(
            P("dp", "ctx", None),
            P("dp", "ctx", None),
            P("dp", None),
            P("dp", None),
            P("dp", None),
            P("dp", None),
            P(None, "dp"),
            P(),
            P(),
            P(),
            P(),
        ),
        out_specs=(P("dp", "ctx", None), P(), P(), P(), P()),
        check_vma=False,
    )
```

```python
import math

import jax
import jax.numpy as jnp
from jax import lax
from jax.experimental import pallas as pl
from jax.experimental.pallas import tpu as pltpu
from jax.sharding import PartitionSpec as P

MESH = pl.DeviceIdType.MESH
NX, NY, NZ = 4, 8, 8
ROWS = 128
WIDTH = 1024
HEADS = 4
HEAD_DIM = 128
HEADS_WIDTH = HEADS * HEAD_DIM
LEFT = 128
TAPS = 9
RIM = 16
EXT = 2 * ROWS + 2 * RIM
CONV = ROWS + 16
DEEP = 64
GROUP = 8
EPSILON = 1e-05
FAR = -1e30
BEFORE = -(1 << 20)
SCALE = HEAD_DIM ** (-0.5)
SLOTS = 176
F32 = jnp.float32
BF16 = jnp.bfloat16

SHARDS = ((-1, 0), (1, 0), (2, 0), (0, 1), (-1, 1), (1, 1), (2, 1), (0, 0))
DIRECT_SHARDS, FAR_SHARDS, OWN = (4, 5, 0, 1), (6, 2), 7
LATER, HALVED, FORWARD = (0, 1, 3), (4, 5, 6, 2), ((4, 0), (5, 0), (6, 0))
RELAYED = {0: (2, 0), 1: (2, 1), 4: (6, 0), 5: (6, 1)}


class Links:
    def __init__(self, send_sems, recv_sems):
        self.send_sems, self.recv_sems = send_sems, recv_sems
        self.names, self.sent = {}, []

    def copy(self, name, source, target, device):
        slot = self.names.setdefault(name, len(self.names))
        assert slot < SLOTS
        return pltpu.make_async_remote_copy(
            src_ref=source,
            dst_ref=target,
            send_sem=self.send_sems.at[slot],
            recv_sem=self.recv_sems.at[slot],
            device_id=device,
            device_id_type=MESH,
        )

    def send(self, name, source, target, device):
        copy = self.copy(name, source, target, device)
        copy.start()
        self.sent.append(copy)

    def arrived(self, name, target, device):
        self.copy(name, target, target, device).wait_recv()

    def finish(self):
        for copy in self.sent:
            copy.wait_send()


def dot(left, right):
    return jnp.dot(left, right, preferred_element_type=F32)


def dot_nt(left, right):
    return lax.dot_general(left, right, (((1,), (1,)), ((), ())), preferred_element_type=F32)


def dot_tn(left, right):
    return lax.dot_general(left, right, (((0,), (0,)), ((), ())), preferred_element_type=F32)


def normalize(values):
    center = values - jnp.mean(values, axis=-1, keepdims=True)
    inverse = lax.rsqrt(jnp.mean(center * center, axis=-1, keepdims=True) + EPSILON)
    return center * inverse, inverse


def wide(column, width):
    return jnp.broadcast_to(column, (column.shape[0], width))


def spread(block):
    return jnp.concatenate([block] * (WIDTH // 128), axis=1)


def iota(shape, axis):
    return lax.broadcasted_iota(jnp.int32, shape, axis)


def block_kernel(
    frames, cotangent, lengths, w_query, w_key, w_value, w_output, att_gain, conv_gain, kernel, bias,
    out_frames, out_sums,
    xs, cts, rims_out, rims_in, weights, gain_a, gain_c, taps_ref, bias_ref,
    norm_b, scaled_a, inverse_a, keys, values, query, query_e, query_n, probs, probs_rim, context, mid,
    scaled_c, inverse_c, conv_in, age, grad_conv, grad_conv_in, grad_mid_norm, grad_mid_b,
    grad_context, grad_context_n, grad_query, grad_key, grad_value, grad_norm_a,
    frames_out, mask_main, mask_rim, mask_next, stats, stats_n, delta, delta_n,
    early, early_x, early_y, early_z, early_all, late_sum, late_x, late_y, late_z,
    sums,
    send_sems, recv_sems, local_sems,
):
    dp, ctx = lax.axis_index("dp"), lax.axis_index("ctx")
    pair = lax.div(dp, 2)
    core = dp - 2 * pair
    y_lo = lax.div(pair, NX)
    x = pair - NX * y_lo
    z = lax.div(ctx, NY // 2)
    y_hi = ctx - (NY // 2) * z
    y = 2 * y_hi + y_lo
    offset = ctx * ROWS
    group = x * 2 + core

    def wrap(value, step, size):
        moved = value + step
        if isinstance(step, int) and step < 0:
            return jnp.where(moved < 0, moved + size, moved)
        return jnp.where(moved >= size, moved - size, moved)

    def flip(bit, change):
        return 1 - bit if change else bit

    def at(px, p_hi, p_lo, pz, pc):
        return ((p_lo * NX + px) * 2 + pc, pz * (NY // 2) + p_hi)

    def frames_at(step):
        return (dp, wrap(ctx, step, NZ * NY // 2))

    sibling = at(x, y_hi, y_lo, z, 1 - core)
    y_below = jnp.where(y_hi + y_lo == 0, NY // 2 - 1, y_hi + y_lo - 1)
    right, left = at(wrap(x, 1, NX), y_hi, y_lo, z, core), at(wrap(x, -1, NX), y_hi, y_lo, z, core)
    y_above = wrap(y_hi, y_lo, NY // 2)
    corners_above = [at(wrap(x, step, NX), y_above, 1 - y_lo, z, core) for step in (-1, 1)]
    corners_below = [at(wrap(x, step, NX), y_below, 1 - y_lo, z, core) for step in (-1, 1)]
    below = at(x, y_below, 1 - y_lo, z, core)
    front, back = at(x, y_hi, y_lo, wrap(z, 1, NZ), core), at(x, y_hi, y_lo, wrap(z, -1, NZ), core)
    later, earlier, later_2 = frames_at(1), frames_at(-1), frames_at(2)

    group_steps, y_steps, z_steps = [], [], []
    for step in (2, 1, -1, 0):
        for change in (1, 0):
            if (step, change) != (0, 0):
                to, of = wrap(x, step, NX), wrap(x, -step, NX)
                pc = flip(core, change)
                group_steps.append(((step, change), to * 2 + pc, at(to, y_hi, y_lo, z, pc), of * 2 + pc))
    for step in (2, -1, 1, 0):
        for change in (1, 0):
            if (step, change) != (0, 0):
                to, of = wrap(y_hi, step, NY // 2), wrap(y_hi, -step, NY // 2)
                lo = flip(y_lo, change)
                y_steps.append(((step, change), to * 2 + lo, at(x, to, lo, z, core), of * 2 + lo))
    for step in (4, 3, -3, 2, -2, 1, -1):
        to, of = wrap(z, step, NZ), wrap(z, -step, NZ)
        z_steps.append((step, to, at(x, y_hi, y_lo, to, core), of))

    links = Links(send_sems, recv_sems)
    local = []

    def bring(source, target):
        copy = pltpu.make_async_copy(source, target, local_sems.at[len(local)])
        copy.start()
        local.append(copy)
        return copy

    barrier = pltpu.get_barrier_semaphore()
    peers = [step[2] for step in z_steps + y_steps + group_steps]
    peers += [later, earlier, later_2, frames_at(-2)]
    peers += corners_above + corners_below
    for peer in peers:
        pl.semaphore_signal(barrier, inc=1, device_id=peer, device_id_type=MESH)

    own_rows = pl.ds(pl.multiple_of(dp * DEEP, DEEP), DEEP)
    got_weights = [
        bring(source, weights.at[index, own_rows, :])
        for index, source in ((0, w_key), (1, w_query), (2, w_value), (3, w_output))
    ]
    got_frames = bring(frames.at[0], xs.at[pl.ds(0, ROWS), :])
    got_rest = [
        bring(cotangent.at[0], cts.at[pl.ds(0, ROWS), :]),
        bring(att_gain, gain_a),
        bring(conv_gain, gain_c),
        bring(kernel, taps_ref),
        bring(bias, bias_ref),
    ]

    for copy in got_weights:
        copy.wait()
    got_frames.wait()
    for copy in got_rest:
        copy.wait()

    def pack(rows):
        return jnp.concatenate([rows[:, : WIDTH // 2], rows[:, WIDTH // 2 :]], axis=0).astype(BF16)

    def unpack(packed):
        rows = packed.astype(F32)
        return jnp.concatenate([rows[:8], rows[8:]], axis=1)

    rims_out[0] = pack(xs[ROWS - RIM : ROWS, :].astype(F32)[8:])
    rims_out[1] = pack(xs[:RIM, :].astype(F32)[:8])
    rims_out[2] = pack(cts[:RIM, :].astype(F32)[:8])
    pl.semaphore_wait(barrier, len(peers))

    half = z - 2 * lax.div(z, 2)

    def shard(index, of_core):
        step, other = SHARDS[index]
        return (flip(y_lo, other) * NX + wrap(x, step, NX)) * 2 + of_core

    def piece(index, of_half, part, wave, of_core):
        first, size = shard(index, of_core) * DEEP, DEEP
        if of_half is not None:
            first, size = first + of_half * 32, 32
        if part is not None:
            first, size = first + part * 16, 16
        return weights.at[:, pl.ds(pl.multiple_of(first, 16), size), :]

    def give(name, index, of_half, part, wave, device):
        ref = piece(index, of_half, part, wave, core)
        links.send((name, wave), ref, ref, device)

    def take(name, index, of_half, part, wave, of_core=None):
        ref = piece(index, of_half, part, wave, core if of_core is None else of_core)
        links.arrived((name, wave), ref, sibling)

    siblings = []

    def pass_on(name, index, of_half, part, wave):
        give("sib" + name, index, of_half, part, wave, sibling)
        siblings.append((name, index, of_half, part, wave))

    targets = {0: right, 1: left, 3: below, 4: corners_below[1], 5: corners_below[0]}

    def give_own(wave):
        for index in DIRECT_SHARDS:
            ref = piece(OWN, half, None, wave, core)
            links.send((str(index), wave), ref, ref, targets[index])
        pass_on("own", OWN, None, None, wave)

    give_own(0)

    links.send("prev", frames.at[0], xs.at[pl.ds(ROWS, ROWS), :], later)
    links.send("prev2", rims_out.at[0], rims_in.at[0], later_2)
    links.send("next", rims_out.at[1], rims_in.at[1], earlier)
    links.send("cot", rims_out.at[2], rims_in.at[2], earlier)

    def norm_rows(first, size, own):
        block = xs[pl.ds(first, size), :].astype(F32)
        scaled, inverse = normalize(block)
        norm_b[pl.ds(first, size), :] = (scaled * gain_a[...]).astype(BF16)
        if own is not None:
            scaled_a[pl.ds(first, size), :] = scaled
        if own:
            inverse_a[pl.ds(first, size), :] = wide(inverse, 128)
            mid[pl.ds(pl.multiple_of(first + 8, 8), size), :] = block
        return block

    @pl.loop(0, 4, unroll=True)
    def _(step):
        norm_rows(pl.multiple_of(step * 32, 32), 32, True)

    ends = [jnp.int32(0)]
    for record in range(lengths.shape[1]):
        ends.append(ends[-1] + lengths[0, record])

    def start_of(places):
        start = jnp.full(places.shape, BEFORE, jnp.int32)
        for end in ends:
            start = jnp.where(places >= end, end, start)
        return start

    def mask_of(query_places, key_places):
        first = jnp.maximum(start_of(query_places), query_places - LEFT)
        return jnp.where((key_places <= query_places) & (key_places >= first), 0.0, FAR).astype(F32)

    square = (ROWS, ROWS)
    place_rows, place_lanes = offset + iota(square, 0), offset + iota(square, 1)
    mask_main[:, :ROWS] = mask_of(place_rows, place_lanes)
    mask_main[:, ROWS:] = mask_of(place_rows, place_lanes - ROWS)
    mask_next[...] = mask_of(place_lanes + ROWS, place_rows)
    rim_rows = iota((16, EXT), 0)
    rim_places = offset + jnp.where(rim_rows < 8, rim_rows - 8, rim_rows + (ROWS - 8))
    lanes = iota((16, EXT), 1)
    rim_keys = jnp.where(lanes < ROWS, lanes, lanes - 2 * ROWS)
    rim_keys = jnp.where(lanes < 2 * ROWS, rim_keys, lanes - (3 * ROWS + RIM))
    rim_keys = offset + jnp.where(lanes < 2 * ROWS + RIM, rim_keys, lanes - (ROWS + RIM))
    mask_rim[...] = mask_of(rim_places, rim_keys)
    age_rows = offset + iota((ROWS + 8, 128), 0)
    age[...] = age_rows - start_of(age_rows)


    def pass_z(index, part, wave):
        give(f"z{part}{index}", index, half, part, wave, front if (index, part) in FORWARD else back)

    for wave in (0,):
        for index in DIRECT_SHARDS:
            take(str(index), index, half, None, wave)
            if index in RELAYED:
                further, part = RELAYED[index]
                give(f"{further}{part}", index, half, part, wave, (right, left)[part])
            if index in HALVED:
                for part in (0, 1):
                    pass_z(index, part, wave)
            pass_on(str(index), index, half, None, wave)
        for index in LATER:
            of_half = None if index == 3 else 1 - half
            ref = piece(OWN, of_half, None, wave, core)
            links.send((f"o{index}", wave), ref, ref, targets[index])
    for wave in (0,):
        for index in FAR_SHARDS:
            for part in (0, 1):
                take(f"{index}{part}", index, half, part, wave)
                pass_z(index, part, wave)
                pass_on(f"{index}{part}", index, half, part, wave)

    def take_rest(wave):
        for index in LATER:
            of_half = None if index == 3 else 1 - half
            take(f"o{index}", index, of_half, None, wave)
            pass_on(f"o{index}", index, of_half, None, wave)
        for index in HALVED:
            for part in (0, 1):
                take(f"z{part}{index}", index, 1 - half, part, wave)
                pass_on(f"z{part}{index}", index, 1 - half, part, wave)

    def take_siblings(of_wave):
        for name, index, of_half, part, wave in siblings:
            if wave == of_wave:
                take("sib" + name, index, of_half, part, wave, 1 - core)

    links.arrived("prev", xs.at[pl.ds(ROWS, ROWS), :], earlier)
    links.arrived("prev2", rims_in.at[0], earlier)
    links.arrived("next", rims_in.at[1], earlier)
    links.arrived("cot", rims_in.at[2], earlier)
    zeros = jnp.zeros((8, WIDTH), F32)
    before, after, cot_after = (unpack(rims_in[index]) for index in range(3))
    xs[2 * ROWS : 2 * ROWS + RIM, :] = jnp.concatenate([zeros, before], axis=0).astype(BF16)
    xs[2 * ROWS + RIM :, :] = jnp.concatenate([after, zeros], axis=0).astype(BF16)
    cts[ROWS:, :] = jnp.concatenate([cot_after, zeros], axis=0).astype(BF16)

    @pl.loop(4, 8, unroll=True)
    def _(step):
        norm_rows(pl.multiple_of(step * 32, 32), 32, False)

    block = norm_rows(2 * ROWS, 2 * RIM, None)
    mid[pl.ds(ROWS + 8, 8), :] = block[RIM : RIM + 8]
    mid[pl.ds(0, 8), :] = xs[pl.ds(2 * ROWS - RIM, RIM), :].astype(F32)[8:]

    take_rest(0)
    take_siblings(0)

    normed = norm_b[...]
    keys[...] = dot(normed, weights[0]).astype(BF16)
    rows = jnp.concatenate(
        [normed[:ROWS], normed[2 * ROWS - RIM : 2 * ROWS], normed[2 * ROWS + RIM :]], axis=0
    )
    projected = dot(rows, weights[1])
    query[...] = projected[:ROWS].astype(BF16)
    query_e[...] = projected[ROWS + 8 : ROWS + 24].astype(BF16)
    links.send("query", query, query_n, earlier)

    def head(index):
        return slice(index * HEAD_DIM, (index + 1) * HEAD_DIM)

    lane = iota(square, 1)
    columns = jnp.zeros(square, F32)
    for h in range(HEADS):
        scores = dot_nt(query[:, head(h)], keys[: 2 * ROWS, head(h)]) * SCALE + mask_main[...]
        top = jnp.max(scores, axis=-1, keepdims=True)
        shifted = jnp.exp(scores - top)
        part = 1.0 / jnp.sum(shifted, axis=-1, keepdims=True)
        probs[h] = shifted * part
        columns = jnp.where(lane == h, top, columns)
        columns = jnp.where(lane == HEADS + h, part, columns)
        scores = dot_nt(query_e[:, head(h)], keys[:, head(h)]) * SCALE + mask_rim[...]
        shifted = jnp.exp(scores - jnp.max(scores, axis=-1, keepdims=True))
        share = shifted * (1.0 / jnp.sum(shifted, axis=-1, keepdims=True))
        probs_rim[h] = share.astype(BF16)
    values[...] = dot(norm_b[...], weights[2]).astype(BF16)
    for h in range(HEADS):
        context[8 : ROWS + 8, head(h)] = dot(probs[h].astype(BF16), values[: 2 * ROWS, head(h)])
        rims = dot(probs_rim[h], values[:, head(h)])
        context[0:8, head(h)] = rims[:8]
        context[ROWS + 8 :, head(h)] = rims[8:]
    stats[...] = columns.T[:8]
    links.send("stats", stats, stats_n, earlier)

    mid[...] += dot_nt(context[...].astype(BF16), weights[3])

    @pl.loop(0, 3, unroll=True)
    def _(step):
        part_rows = pl.ds(pl.multiple_of(step * 48, 8), 48)
        scaled, inverse = normalize(mid[part_rows, :])
        scaled_c[part_rows, :] = scaled
        inverse_c[part_rows, :] = wide(inverse, 128)
        normed = (scaled * gain_c[...]).astype(BF16).astype(F32)
        for tile in range(WIDTH // 128):
            conv_in[tile, part_rows, :] = normed[:, tile * 128 : (tile + 1) * 128]

    @pl.loop(0, WIDTH // 128)
    def _(tile):
        part_lanes = pl.ds(pl.multiple_of(tile * 128, 128), 128)
        conv = jnp.broadcast_to(bias_ref[:, part_lanes], (ROWS + 8, 128))
        for back_by in range(TAPS):
            term = conv_in[tile, pl.ds(8 - back_by, ROWS + 8), :]
            term = term * taps_ref[TAPS - 1 - back_by : TAPS - back_by, part_lanes]
            conv = conv + jnp.where(age[...] >= back_by, term, 0.0)
        gate = 1.0 / (1.0 + jnp.exp(-conv))
        grad_out = cts[:, part_lanes].astype(F32)[: ROWS + 8]
        grad = grad_out * gate * (1.0 + conv * (1.0 - gate))
        grad_conv[...] = grad
        grad = grad[:ROWS]
        early[tile, 9:10, :] = jnp.sum(grad, axis=0, keepdims=True)
        total = jnp.zeros((ROWS, 128), F32)
        for back_by in range(TAPS):
            tap = TAPS - 1 - back_by
            kept = jnp.where(age[:ROWS, :] >= back_by, grad, 0.0)
            term = kept * conv_in[tile, pl.ds(8 - back_by, ROWS), :]
            early[tile, tap : tap + 1, :] = jnp.sum(term, axis=0, keepdims=True)
            ahead = pl.ds(back_by, ROWS)
            kept = jnp.where(age[ahead, :] >= back_by, grad_conv[ahead, :], 0.0)
            total = total + kept * taps_ref[tap : tap + 1, part_lanes]
        grad_conv_in[:, part_lanes] = total
        term = total * scaled_c[8 : ROWS + 8, part_lanes]
        early[tile, 10:11, :] = jnp.sum(term, axis=0, keepdims=True)
        early[tile, 11:16, :] = jnp.zeros((5, 128), F32)

    def spread_out(name, slots, me, steps):
        for step, _, device, _ in steps:
            links.send((name, step), slots.at[me], slots.at[me], device)

    def collect(name, slots, steps):
        for step, _, _, source in steps:
            links.arrived((name, step), slots.at[source], sibling)
        total = slots[0]
        for index in range(1, slots.shape[0]):
            total = total + slots[index]
        return total

    early_x[group] = early[group]
    for step, other, device, _ in group_steps:
        links.send(("ex", step), early.at[other], early_x.at[group], device)

    @pl.loop(0, 4, unroll=True)
    def _(step):
        part_rows = pl.ds(pl.multiple_of(step * 32, 32), 32)
        ext_rows = pl.ds(pl.multiple_of(step * 32 + 8, 8), 32)
        grad, scaled = grad_conv_in[part_rows, :] * gain_c[...], scaled_c[ext_rows, :]
        first = jnp.mean(grad, axis=-1, keepdims=True)
        second = jnp.mean(grad * scaled, axis=-1, keepdims=True)
        result = spread(inverse_c[ext_rows, :]) * (grad - first - scaled * second)
        grad_mid_norm[part_rows, :] = result
        grad_mid_b[part_rows, :] = (cts[part_rows, :].astype(F32) + result).astype(BF16)

    grad_context[...] = dot(grad_mid_b[...], weights[3]).astype(BF16)
    links.send("grad", grad_context, grad_context_n, earlier)
    deltas = []
    for h in range(HEADS):
        term = context[8 : ROWS + 8, head(h)] * grad_context[:, head(h)].astype(F32)
        deltas.append(jnp.sum(term, axis=-1, keepdims=True))

    for h in range(HEADS):
        grad_h = grad_context[:, head(h)]
        share = probs[h]
        grad_probs = dot_nt(grad_h, values[: 2 * ROWS, head(h)])
        grad_scores = (share * (grad_probs - deltas[h]) * SCALE).astype(BF16)
        grad_query[:, head(h)] = dot(grad_scores, keys[: 2 * ROWS, head(h)]).astype(BF16)
        grad_key[:, head(h)] = dot_tn(grad_scores, query[:, head(h)]).astype(BF16)
        grad_value[:, head(h)] = dot_tn(share.astype(BF16), grad_h).astype(BF16)

    parts = dot_nt(grad_key[...], weights[0]) + dot_nt(grad_value[...], weights[2])
    own_part = parts[:ROWS] + dot_nt(grad_query[...], weights[1])
    grad_norm_a[...] = own_part
    product = own_part * scaled_a[:ROWS] + parts[ROWS:] * scaled_a[ROWS:]
    total = jnp.sum(product, axis=0, keepdims=True)
    for tile in range(WIDTH // 128):
        late_sum[tile : tile + 1, :] = total[:, tile * 128 : (tile + 1) * 128]
    late_x[group] = late_sum[...]
    spread_out("lx", late_x, group, group_steps)

    columns = jnp.zeros(square, F32)
    for h in range(HEADS):
        columns = jnp.where(lane == h, deltas[h], columns)
    delta[...] = columns.T[:8]
    links.send("delta", delta, delta_n, earlier)

    early_z[z] = collect("ex", early_x, group_steps)
    spread_out("ez", early_z, z, z_steps)
    late_z[z] = collect("lx", late_x, group_steps)
    spread_out("lz", late_z, z, z_steps)
    early_y[y] = collect("ez", early_z, z_steps)
    spread_out("ey", early_y, y, y_steps)

    links.arrived("query", query_n, earlier)
    links.arrived("stats", stats_n, earlier)
    links.arrived("grad", grad_context_n, earlier)
    links.arrived("delta", delta_n, earlier)
    for h in range(HEADS):
        query_h, grad_h = query_n[:, head(h)], grad_context_n[:, head(h)]
        scores = dot_nt(keys[:ROWS, head(h)], query_h) * SCALE + mask_next[...]
        share = jnp.exp(scores - stats_n[h : h + 1, :]) * stats_n[HEADS + h : HEADS + h + 1, :]
        grad_probs = dot_nt(values[:ROWS, head(h)], grad_h)
        grad_scores = (share * (grad_probs - delta_n[h : h + 1, :]) * SCALE).astype(BF16)
        grad_key[:ROWS, head(h)] = dot(grad_scores, query_h).astype(BF16)
        grad_value[:ROWS, head(h)] = dot(share.astype(BF16), grad_h).astype(BF16)

    late_y[y] = collect("lz", late_z, z_steps)
    spread_out("ly", late_y, y, y_steps)
    early_all[group] = collect("ey", early_y, y_steps)
    spread_out("ea", early_all, group, group_steps)

    grad_norm_a[...] += dot_nt(grad_key[:ROWS], weights[0]) + dot_nt(grad_value[:ROWS], weights[2])

    @pl.loop(0, 4, unroll=True)
    def _(step):
        part_rows = pl.ds(pl.multiple_of(step * 32, 32), 32)
        grad, scaled = grad_norm_a[part_rows, :] * gain_a[...], scaled_a[part_rows, :]
        first = jnp.mean(grad, axis=-1, keepdims=True)
        second = jnp.mean(grad * scaled, axis=-1, keepdims=True)
        result = spread(inverse_a[part_rows, :]) * (grad - first - scaled * second)
        frames_out[part_rows, :] = grad_mid_norm[part_rows, :] + result

    out_copy = bring(frames_out, out_frames.at[0])
    links.finish()

    factor = 1.0 / math.sqrt(NX * 2 * 2 * (NY // 2) * NZ * ROWS)
    for step, _, _, source in group_steps:
        links.arrived(("ea", step), early_all.at[source], sibling)
    for tile in range(WIDTH // 128):
        sums[:, tile * 128 : (tile + 1) * 128] = early_all[tile] * factor
    summed = collect("ly", late_y, y_steps) * factor
    for tile in range(WIDTH // 128):
        sums[11:12, tile * 128 : (tile + 1) * 128] = summed[tile : tile + 1]
    bring(sums, out_sums).wait()
    out_copy.wait()


def finish_kernel(frames_in, sums, out_frames, out_att, out_conv, out_kernel, out_bias):
    out_frames[...] = frames_in[...]

    @pl.when(pl.program_id(0) == 0)
    def _():
        out_kernel[...] = sums[:TAPS]
        out_bias[...] = sums[9:10]
        out_conv[...] = sums[10:11]
        out_att[...] = sums[11:12]


def scratch():
    def buffer(*shape, dtype=F32):
        return pltpu.VMEM(shape, dtype)

    return [
        buffer(EXT, WIDTH, dtype=BF16),
        buffer(CONV, WIDTH, dtype=BF16),
        buffer(3, 16, WIDTH // 2, dtype=BF16),
        buffer(3, 16, WIDTH // 2, dtype=BF16),
        buffer(4, WIDTH, HEADS_WIDTH, dtype=BF16),
        buffer(1, WIDTH),
        buffer(1, WIDTH),
        buffer(TAPS, WIDTH),
        buffer(1, WIDTH),
        buffer(EXT, WIDTH, dtype=BF16),
        buffer(2 * ROWS, WIDTH),
        buffer(ROWS, 128),
        buffer(EXT, HEADS_WIDTH, dtype=BF16),
        buffer(EXT, HEADS_WIDTH, dtype=BF16),
        buffer(ROWS, HEADS_WIDTH, dtype=BF16),
        buffer(16, HEADS_WIDTH, dtype=BF16),
        buffer(ROWS, HEADS_WIDTH, dtype=BF16),
        buffer(HEADS, ROWS, 2 * ROWS),
        buffer(HEADS, 16, EXT, dtype=BF16),
        buffer(CONV, HEADS_WIDTH),
        buffer(CONV, WIDTH),
        buffer(CONV, WIDTH),
        buffer(CONV, 128),
        buffer(WIDTH // 128, CONV, 128),
        buffer(ROWS + 8, 128, dtype=jnp.int32),
        buffer(ROWS + 8, 128),
        buffer(ROWS, WIDTH),
        buffer(ROWS, WIDTH),
        buffer(ROWS, WIDTH, dtype=BF16),
        buffer(ROWS, HEADS_WIDTH, dtype=BF16),
        buffer(ROWS, HEADS_WIDTH, dtype=BF16),
        buffer(ROWS, HEADS_WIDTH, dtype=BF16),
        buffer(2 * ROWS, HEADS_WIDTH, dtype=BF16),
        buffer(2 * ROWS, HEADS_WIDTH, dtype=BF16),
        buffer(ROWS, WIDTH),
        buffer(ROWS, WIDTH),
        buffer(ROWS, 2 * ROWS),
        buffer(16, EXT),
        buffer(ROWS, ROWS),
        buffer(8, 128),
        buffer(8, 128),
        buffer(8, 128),
        buffer(8, 128),
        buffer(GROUP, 16, 128),
        buffer(GROUP, 16, 128),
        buffer(NY, 16, 128),
        buffer(NZ, 16, 128),
        buffer(GROUP, 16, 128),
        buffer(8, 128),
        buffer(GROUP, 8, 128),
        buffer(NY, 8, 128),
        buffer(NZ, 8, 128),
        buffer(16, WIDTH),
        pltpu.SemaphoreType.DMA((SLOTS,)),
        pltpu.SemaphoreType.DMA((SLOTS,)),
        pltpu.SemaphoreType.DMA((16,)),
    ]


def shards(
    frames, cotangent, lengths, w_query, w_key, w_value, w_output, att_gain, conv_gain, kernel, conv_bias
):
    row = (1, WIDTH)
    anywhere = pl.BlockSpec(memory_space=pl.ANY)
    in_specs = [anywhere] * 11
    in_specs[2] = pl.BlockSpec(memory_space=pltpu.SMEM)
    frames_sum, sums = pl.pallas_call(
        block_kernel,
        out_shape=(
            jax.ShapeDtypeStruct(frames.shape, F32),
            jax.ShapeDtypeStruct((16, WIDTH), F32),
        ),
        in_specs=in_specs,
        out_specs=(anywhere,) * 2,
        scratch_shapes=scratch(),
        compiler_params=pltpu.CompilerParams(
            collective_id=0, has_side_effects=True, vmem_limit_bytes=63 << 20
        ),
        cost_estimate=pl.CostEstimate(
            flops=3 << 30, bytes_accessed=4 << 20, transcendentals=1 << 20
        ),
    )(
        frames, cotangent, lengths, w_query, w_key, w_value, w_output.T,
        att_gain.reshape(row), conv_gain.reshape(row), kernel, conv_bias.reshape(row),
    )
    steps = 2
    moving = pl.BlockSpec((1, ROWS // steps, WIDTH), lambda step: (0, step, 0))

    def fixed(rows):
        return pl.BlockSpec((rows, WIDTH), lambda step: (0, 0))

    grad_frames, grad_att, grad_conv, grad_kernel, grad_bias = pl.pallas_call(
        finish_kernel,
        grid=(steps,),
        out_shape=(
            jax.ShapeDtypeStruct(frames.shape, F32),
            jax.ShapeDtypeStruct(row, F32),
            jax.ShapeDtypeStruct(row, F32),
            jax.ShapeDtypeStruct(kernel.shape, F32),
            jax.ShapeDtypeStruct(row, F32),
        ),
        in_specs=[moving, fixed(16)],
        out_specs=(moving, fixed(1), fixed(1), fixed(TAPS), fixed(1)),
        compiler_params=pltpu.CompilerParams(vmem_limit_bytes=63 << 20),
    )(frames_sum, sums)
    return (
        grad_frames,
        grad_att.reshape(WIDTH),
        grad_conv.reshape(WIDTH),
        grad_kernel,
        grad_bias.reshape(WIDTH),
    )


def solution(mesh):
    return jax.shard_map(
        shards,
        mesh=mesh,
        in_specs=(
            P("dp", "ctx", None),
            P("dp", "ctx", None),
            P("dp", None),
            P("dp", None),
            P("dp", None),
            P("dp", None),
            P(None, "dp"),
            P(),
            P(),
            P(),
            P(),
        ),
        out_specs=(P("dp", "ctx", None), P(), P(), P(), P()),
        check_vma=False,
    )
```

```python
import math

import jax
import jax.numpy as jnp
from jax import lax
from jax.experimental import pallas as pl
from jax.experimental.pallas import tpu as pltpu
from jax.sharding import PartitionSpec as P

MESH = pl.DeviceIdType.MESH
NX, NY, NZ = 4, 8, 8
ROWS = 128
WIDTH = 1024
HEADS = 4
HEAD_DIM = 128
HEADS_WIDTH = HEADS * HEAD_DIM
LEFT = 128
TAPS = 9
RIM = 16
EXT = 2 * ROWS + 2 * RIM
CONV = ROWS + 16
DEEP = 64
GROUP = 8
EPSILON = 1e-05
FAR = -1e30
BEFORE = -(1 << 20)
SCALE = HEAD_DIM ** (-0.5)
SLOTS = 176
F32 = jnp.float32
BF16 = jnp.bfloat16

SHARDS = ((-1, 0), (1, 0), (2, 0), (0, 1), (-1, 1), (1, 1), (2, 1), (0, 0))
DIRECT_SHARDS, FAR_SHARDS, OWN = (4, 5, 0, 1), (6, 2), 7
LATER, HALVED, FORWARD = (0, 1, 3), (4, 5, 6, 2), ((4, 0), (5, 0), (6, 0))
RELAYED = {0: (2, 0), 1: (2, 1), 4: (6, 0), 5: (6, 1)}


class Links:
    def __init__(self, send_sems, recv_sems):
        self.send_sems, self.recv_sems = send_sems, recv_sems
        self.names, self.sent = {}, []

    def copy(self, name, source, target, device):
        slot = self.names.setdefault(name, len(self.names))
        assert slot < SLOTS
        return pltpu.make_async_remote_copy(
            src_ref=source,
            dst_ref=target,
            send_sem=self.send_sems.at[slot],
            recv_sem=self.recv_sems.at[slot],
            device_id=device,
            device_id_type=MESH,
        )

    def send(self, name, source, target, device):
        copy = self.copy(name, source, target, device)
        copy.start()
        self.sent.append(copy)

    def arrived(self, name, target, device):
        self.copy(name, target, target, device).wait_recv()

    def finish(self):
        for copy in self.sent:
            copy.wait_send()


def dot(left, right):
    return jnp.dot(left, right, preferred_element_type=F32)


def dot_nt(left, right):
    return lax.dot_general(left, right, (((1,), (1,)), ((), ())), preferred_element_type=F32)


def dot_tn(left, right):
    return lax.dot_general(left, right, (((0,), (0,)), ((), ())), preferred_element_type=F32)


def normalize(values):
    center = values - jnp.mean(values, axis=-1, keepdims=True)
    inverse = lax.rsqrt(jnp.mean(center * center, axis=-1, keepdims=True) + EPSILON)
    return center * inverse, inverse


def wide(column, width):
    return jnp.broadcast_to(column, (column.shape[0], width))


def spread(block):
    return jnp.concatenate([block] * (WIDTH // 128), axis=1)


def iota(shape, axis):
    return lax.broadcasted_iota(jnp.int32, shape, axis)


def block_kernel(
    frames, cotangent, lengths, w_query, w_key, w_value, w_output, att_gain, conv_gain, kernel, bias,
    out_frames, out_sums,
    xs, cts, rims_out, rims_in, weights, gain_a, gain_c, taps_ref, bias_ref,
    norm_b, scaled_a, inverse_a, keys, values, query, query_e, query_n, probs, probs_rim, context, mid,
    scaled_c, inverse_c, conv_in, age, grad_conv, grad_conv_in, grad_mid_norm, grad_mid_b,
    grad_context, grad_context_n, grad_query, grad_key, grad_value, grad_norm_a,
    frames_out, mask_main, mask_rim, mask_next, stats, stats_n,
    early, early_b, early_x, early_y, early_z, early_all, late_sum, late_x, late_y, late_z,
    sums,
    send_sems, recv_sems, local_sems,
):
    dp, ctx = lax.axis_index("dp"), lax.axis_index("ctx")
    pair = lax.div(dp, 2)
    core = dp - 2 * pair
    y_lo = lax.div(pair, NX)
    x = pair - NX * y_lo
    z = lax.div(ctx, NY // 2)
    y_hi = ctx - (NY // 2) * z
    y = 2 * y_hi + y_lo
    offset = ctx * ROWS
    group = x * 2 + core

    def wrap(value, step, size):
        moved = value + step
        if isinstance(step, int) and step < 0:
            return jnp.where(moved < 0, moved + size, moved)
        return jnp.where(moved >= size, moved - size, moved)

    def flip(bit, change):
        return 1 - bit if change else bit

    def at(px, p_hi, p_lo, pz, pc):
        return ((p_lo * NX + px) * 2 + pc, pz * (NY // 2) + p_hi)

    def frames_at(step):
        return (dp, wrap(ctx, step, NZ * NY // 2))

    sibling = at(x, y_hi, y_lo, z, 1 - core)
    y_below = jnp.where(y_hi + y_lo == 0, NY // 2 - 1, y_hi + y_lo - 1)
    right, left = at(wrap(x, 1, NX), y_hi, y_lo, z, core), at(wrap(x, -1, NX), y_hi, y_lo, z, core)
    y_above = wrap(y_hi, y_lo, NY // 2)
    corners_above = [at(wrap(x, step, NX), y_above, 1 - y_lo, z, core) for step in (-1, 1)]
    corners_below = [at(wrap(x, step, NX), y_below, 1 - y_lo, z, core) for step in (-1, 1)]
    below = at(x, y_below, 1 - y_lo, z, core)
    front, back = at(x, y_hi, y_lo, wrap(z, 1, NZ), core), at(x, y_hi, y_lo, wrap(z, -1, NZ), core)
    later, earlier, later_2 = frames_at(1), frames_at(-1), frames_at(2)

    group_steps, y_steps, z_steps = [], [], []
    for step in (2, 1, -1, 0):
        for change in (1, 0):
            if (step, change) != (0, 0):
                to, of = wrap(x, step, NX), wrap(x, -step, NX)
                pc = flip(core, change)
                group_steps.append(((step, change), to * 2 + pc, at(to, y_hi, y_lo, z, pc), of * 2 + pc))
    for step in (2, -1, 1, 0):
        for change in (1, 0):
            if (step, change) != (0, 0):
                to, of = wrap(y_hi, step, NY // 2), wrap(y_hi, -step, NY // 2)
                lo = flip(y_lo, change)
                y_steps.append(((step, change), to * 2 + lo, at(x, to, lo, z, core), of * 2 + lo))
    for step in (4, 3, -3, 2, -2, 1, -1):
        to, of = wrap(z, step, NZ), wrap(z, -step, NZ)
        z_steps.append((step, to, at(x, y_hi, y_lo, to, core), of))

    links = Links(send_sems, recv_sems)
    local = []

    def bring(source, target):
        copy = pltpu.make_async_copy(source, target, local_sems.at[len(local)])
        copy.start()
        local.append(copy)
        return copy

    barrier = pltpu.get_barrier_semaphore()
    peers = [step[2] for step in z_steps + y_steps + group_steps]
    peers += [later, earlier, later_2, frames_at(-2)]
    peers += corners_above + corners_below
    for peer in peers:
        pl.semaphore_signal(barrier, inc=1, device_id=peer, device_id_type=MESH)

    own_rows = pl.ds(pl.multiple_of(dp * DEEP, DEEP), DEEP)
    got_weights = [
        bring(source, weights.at[index, own_rows, :])
        for index, source in ((0, w_key), (1, w_query), (2, w_value), (3, w_output))
    ]
    got_frames = bring(frames.at[0], xs.at[pl.ds(0, ROWS), :])
    got_rest = [
        bring(cotangent.at[0], cts.at[pl.ds(0, ROWS), :]),
        bring(att_gain, gain_a),
        bring(conv_gain, gain_c),
        bring(kernel, taps_ref),
        bring(bias, bias_ref),
    ]

    for copy in got_weights:
        copy.wait()
    got_frames.wait()
    for copy in got_rest:
        copy.wait()

    def pack(rows):
        return jnp.concatenate([rows[:, : WIDTH // 2], rows[:, WIDTH // 2 :]], axis=0).astype(BF16)

    def unpack(packed):
        rows = packed.astype(F32)
        return jnp.concatenate([rows[:8], rows[8:]], axis=1)

    rims_out[0] = pack(xs[ROWS - RIM : ROWS, :].astype(F32)[8:])
    rims_out[1] = pack(xs[:RIM, :].astype(F32)[:8])
    rims_out[2] = pack(cts[:RIM, :].astype(F32)[:8])
    pl.semaphore_wait(barrier, len(peers))

    half = z - 2 * lax.div(z, 2)

    def shard(index, of_core):
        step, other = SHARDS[index]
        return (flip(y_lo, other) * NX + wrap(x, step, NX)) * 2 + of_core

    def piece(index, of_half, part, wave, of_core):
        first, size = shard(index, of_core) * DEEP, DEEP
        if of_half is not None:
            first, size = first + of_half * 32, 32
        if part is not None:
            first, size = first + part * 16, 16
        return weights.at[:, pl.ds(pl.multiple_of(first, 16), size), :]

    def give(name, index, of_half, part, wave, device):
        ref = piece(index, of_half, part, wave, core)
        links.send((name, wave), ref, ref, device)

    def take(name, index, of_half, part, wave, of_core=None):
        ref = piece(index, of_half, part, wave, core if of_core is None else of_core)
        links.arrived((name, wave), ref, sibling)

    siblings = []

    def pass_on(name, index, of_half, part, wave):
        give("sib" + name, index, of_half, part, wave, sibling)
        siblings.append((name, index, of_half, part, wave))

    targets = {0: right, 1: left, 3: below, 4: corners_below[1], 5: corners_below[0]}

    def give_own(wave):
        for index in DIRECT_SHARDS:
            ref = piece(OWN, half, None, wave, core)
            links.send((str(index), wave), ref, ref, targets[index])
        pass_on("own", OWN, None, None, wave)

    give_own(0)

    links.send("prev", frames.at[0], xs.at[pl.ds(ROWS, ROWS), :], later)
    links.send("prev2", rims_out.at[0], rims_in.at[0], later_2)
    links.send("next", rims_out.at[1], rims_in.at[1], earlier)
    links.send("cot", rims_out.at[2], rims_in.at[2], earlier)

    def norm_rows(first, size, own):
        block = xs[pl.ds(first, size), :].astype(F32)
        scaled, inverse = normalize(block)
        norm_b[pl.ds(first, size), :] = (scaled * gain_a[...]).astype(BF16)
        if own is not None:
            scaled_a[pl.ds(first, size), :] = scaled
        if own:
            inverse_a[pl.ds(first, size), :] = wide(inverse, 128)
            mid[pl.ds(pl.multiple_of(first + 8, 8), size), :] = block
        return block

    @pl.loop(0, 4, unroll=True)
    def _(step):
        norm_rows(pl.multiple_of(step * 32, 32), 32, True)

    ends = [jnp.int32(0)]
    for record in range(lengths.shape[1]):
        ends.append(ends[-1] + lengths[0, record])

    def start_of(places):
        start = jnp.full(places.shape, BEFORE, jnp.int32)
        for end in ends:
            start = jnp.where(places >= end, end, start)
        return start

    def mask_of(query_places, key_places):
        first = jnp.maximum(start_of(query_places), query_places - LEFT)
        return jnp.where((key_places <= query_places) & (key_places >= first), 0.0, FAR).astype(F32)

    square = (ROWS, ROWS)
    place_rows, place_lanes = offset + iota(square, 0), offset + iota(square, 1)
    mask_main[:, :ROWS] = mask_of(place_rows, place_lanes)
    mask_main[:, ROWS:] = mask_of(place_rows, place_lanes - ROWS)
    mask_next[...] = mask_of(place_lanes + ROWS, place_rows)
    rim_rows = iota((16, EXT), 0)
    rim_places = offset + jnp.where(rim_rows < 8, rim_rows - 8, rim_rows + (ROWS - 8))
    lanes = iota((16, EXT), 1)
    rim_keys = jnp.where(lanes < ROWS, lanes, lanes - 2 * ROWS)
    rim_keys = jnp.where(lanes < 2 * ROWS, rim_keys, lanes - (3 * ROWS + RIM))
    rim_keys = offset + jnp.where(lanes < 2 * ROWS + RIM, rim_keys, lanes - (ROWS + RIM))
    mask_rim[...] = mask_of(rim_places, rim_keys)
    age_rows = offset + iota((ROWS + 8, 128), 0)
    age[...] = age_rows - start_of(age_rows)


    def pass_z(index, part, wave):
        give(f"z{part}{index}", index, half, part, wave, front if (index, part) in FORWARD else back)

    for wave in (0,):
        for index in DIRECT_SHARDS:
            take(str(index), index, half, None, wave)
            if index in RELAYED:
                further, part = RELAYED[index]
                give(f"{further}{part}", index, half, part, wave, (right, left)[part])
            if index in HALVED:
                for part in (0, 1):
                    pass_z(index, part, wave)
            pass_on(str(index), index, half, None, wave)
        for index in LATER:
            of_half = None if index == 3 else 1 - half
            ref = piece(OWN, of_half, None, wave, core)
            links.send((f"o{index}", wave), ref, ref, targets[index])
    for wave in (0,):
        for index in FAR_SHARDS:
            for part in (0, 1):
                take(f"{index}{part}", index, half, part, wave)
                pass_z(index, part, wave)
                pass_on(f"{index}{part}", index, half, part, wave)

    def take_rest(wave):
        for index in LATER:
            of_half = None if index == 3 else 1 - half
            take(f"o{index}", index, of_half, None, wave)
            pass_on(f"o{index}", index, of_half, None, wave)
        for index in HALVED:
            for part in (0, 1):
                take(f"z{part}{index}", index, 1 - half, part, wave)
                pass_on(f"z{part}{index}", index, 1 - half, part, wave)

    def take_siblings(of_wave):
        for name, index, of_half, part, wave in siblings:
            if wave == of_wave:
                take("sib" + name, index, of_half, part, wave, 1 - core)

    take_rest(0)

    links.arrived("prev", xs.at[pl.ds(ROWS, ROWS), :], earlier)
    links.arrived("prev2", rims_in.at[0], earlier)
    links.arrived("next", rims_in.at[1], earlier)
    links.arrived("cot", rims_in.at[2], earlier)
    zeros = jnp.zeros((8, WIDTH), F32)
    before, after, cot_after = (unpack(rims_in[index]) for index in range(3))
    xs[2 * ROWS : 2 * ROWS + RIM, :] = jnp.concatenate([zeros, before], axis=0).astype(BF16)
    xs[2 * ROWS + RIM :, :] = jnp.concatenate([after, zeros], axis=0).astype(BF16)
    cts[ROWS:, :] = jnp.concatenate([cot_after, zeros], axis=0).astype(BF16)

    @pl.loop(4, 8, unroll=True)
    def _(step):
        norm_rows(pl.multiple_of(step * 32, 32), 32, False)

    block = norm_rows(2 * ROWS, 2 * RIM, None)
    mid[pl.ds(ROWS + 8, 8), :] = block[RIM : RIM + 8]
    mid[pl.ds(0, 8), :] = xs[pl.ds(2 * ROWS - RIM, RIM), :].astype(F32)[8:]

    take_siblings(0)

    normed = norm_b[...]
    keys[...] = dot(normed, weights[0]).astype(BF16)
    rows = jnp.concatenate(
        [normed[:ROWS], normed[2 * ROWS - RIM : 2 * ROWS], normed[2 * ROWS + RIM :]], axis=0
    )
    projected = dot(rows, weights[1])
    query[...] = projected[:ROWS].astype(BF16)
    query_e[...] = projected[ROWS + 8 : ROWS + 24].astype(BF16)
    links.send("query", query, query_n, earlier)

    def head(index):
        return slice(index * HEAD_DIM, (index + 1) * HEAD_DIM)

    tops, shares = [], []
    for h in range(HEADS):
        scores = dot_nt(query[:, head(h)], keys[: 2 * ROWS, head(h)]) * SCALE + mask_main[...]
        top = jnp.max(scores, axis=-1, keepdims=True)
        shifted = jnp.exp(scores - top)
        part = 1.0 / jnp.sum(shifted, axis=-1, keepdims=True)
        probs[h] = shifted * part
        tops.append(top)
        shares.append(part)
        scores = dot_nt(query_e[:, head(h)], keys[:, head(h)]) * SCALE + mask_rim[...]
        shifted = jnp.exp(scores - jnp.max(scores, axis=-1, keepdims=True))
        share = shifted * (1.0 / jnp.sum(shifted, axis=-1, keepdims=True))
        probs_rim[h] = share.astype(BF16)
    values[...] = dot(norm_b[...], weights[2]).astype(BF16)
    for h in range(HEADS):
        context[8 : ROWS + 8, head(h)] = dot(probs[h].astype(BF16), values[: 2 * ROWS, head(h)])
        rims = dot(probs_rim[h], values[:, head(h)])
        context[0:8, head(h)] = rims[:8]
        context[ROWS + 8 :, head(h)] = rims[8:]

    mid[...] += dot_nt(context[...].astype(BF16), weights[3])

    @pl.loop(0, 3, unroll=True)
    def _(step):
        part_rows = pl.ds(pl.multiple_of(step * 48, 8), 48)
        scaled, inverse = normalize(mid[part_rows, :])
        scaled_c[part_rows, :] = scaled
        inverse_c[part_rows, :] = wide(inverse, 128)
        normed = (scaled * gain_c[...]).astype(BF16).astype(F32)
        for tile in range(WIDTH // 128):
            conv_in[tile, part_rows, :] = normed[:, tile * 128 : (tile + 1) * 128]

    @pl.loop(0, WIDTH // 128)
    def _(tile):
        part_lanes = pl.ds(pl.multiple_of(tile * 128, 128), 128)
        conv = jnp.broadcast_to(bias_ref[:, part_lanes], (ROWS + 8, 128))
        for back_by in range(TAPS):
            term = conv_in[tile, pl.ds(8 - back_by, ROWS + 8), :]
            term = term * taps_ref[TAPS - 1 - back_by : TAPS - back_by, part_lanes]
            conv = conv + jnp.where(age[...] >= back_by, term, 0.0)
        gate = 1.0 / (1.0 + jnp.exp(-conv))
        grad_out = cts[:, part_lanes].astype(F32)[: ROWS + 8]
        grad = grad_out * gate * (1.0 + conv * (1.0 - gate))
        grad_conv[...] = grad
        grad = grad[:ROWS]
        early[tile, 9:10, :] = jnp.sum(grad, axis=0, keepdims=True)
        total = jnp.zeros((ROWS, 128), F32)
        for back_by in range(TAPS):
            tap = TAPS - 1 - back_by
            kept = jnp.where(age[:ROWS, :] >= back_by, grad, 0.0)
            term = kept * conv_in[tile, pl.ds(8 - back_by, ROWS), :]
            early[tile, tap : tap + 1, :] = jnp.sum(term, axis=0, keepdims=True)
            ahead = pl.ds(back_by, ROWS)
            kept = jnp.where(age[ahead, :] >= back_by, grad_conv[ahead, :], 0.0)
            total = total + kept * taps_ref[tap : tap + 1, part_lanes]
        grad_conv_in[:, part_lanes] = total
        term = total * scaled_c[8 : ROWS + 8, part_lanes]
        early[tile, 10:11, :] = jnp.sum(term, axis=0, keepdims=True)
        early[tile, 11:16, :] = jnp.zeros((5, 128), F32)

    def spread_out(name, slots, me, steps):
        for step, _, device, _ in steps:
            links.send((name, step), slots.at[me], slots.at[me], device)

    def collect(name, slots, steps):
        for step, _, _, source in steps:
            links.arrived((name, step), slots.at[source], sibling)
        total = slots[0].astype(F32)
        for index in range(1, slots.shape[0]):
            total = total + slots[index].astype(F32)
        return total

    early_b[...] = early[...].astype(BF16)
    early_x[group] = early_b[group]
    for step, other, device, _ in group_steps:
        links.send(("ex", step), early_b.at[other], early_x.at[group], device)

    @pl.loop(0, 4, unroll=True)
    def _(step):
        part_rows = pl.ds(pl.multiple_of(step * 32, 32), 32)
        ext_rows = pl.ds(pl.multiple_of(step * 32 + 8, 8), 32)
        grad, scaled = grad_conv_in[part_rows, :] * gain_c[...], scaled_c[ext_rows, :]
        first = jnp.mean(grad, axis=-1, keepdims=True)
        second = jnp.mean(grad * scaled, axis=-1, keepdims=True)
        result = spread(inverse_c[ext_rows, :]) * (grad - first - scaled * second)
        grad_mid_norm[part_rows, :] = result
        grad_mid_b[part_rows, :] = (cts[part_rows, :].astype(F32) + result).astype(BF16)

    grad_context[...] = dot(grad_mid_b[...], weights[3]).astype(BF16)
    links.send("grad", grad_context, grad_context_n, earlier)
    deltas = []
    for h in range(HEADS):
        term = context[8 : ROWS + 8, head(h)] * grad_context[:, head(h)].astype(F32)
        deltas.append(jnp.sum(term, axis=-1, keepdims=True))

    for h in range(HEADS):
        grad_h = grad_context[:, head(h)]
        share = probs[h]
        grad_probs = dot_nt(grad_h, values[: 2 * ROWS, head(h)])
        grad_scores = (share * (grad_probs - deltas[h]) * SCALE).astype(BF16)
        grad_query[:, head(h)] = dot(grad_scores, keys[: 2 * ROWS, head(h)]).astype(BF16)
        grad_key[:, head(h)] = dot_tn(grad_scores, query[:, head(h)]).astype(BF16)
        grad_value[:, head(h)] = dot_tn(share.astype(BF16), grad_h).astype(BF16)

    parts = dot_nt(grad_key[...], weights[0]) + dot_nt(grad_value[...], weights[2])
    own_part = parts[:ROWS] + dot_nt(grad_query[...], weights[1])
    grad_norm_a[...] = own_part
    product = own_part * scaled_a[:ROWS] + parts[ROWS:] * scaled_a[ROWS:]
    total = jnp.sum(product, axis=0, keepdims=True)
    for tile in range(WIDTH // 128):
        late_sum[tile : tile + 1, :] = total[:, tile * 128 : (tile + 1) * 128]
    late_x[group] = late_sum[...]
    spread_out("lx", late_x, group, group_steps)

    lane = iota(square, 1)
    columns = jnp.zeros(square, F32)
    for index, column in enumerate(tops + shares + deltas):
        columns = jnp.where(lane == index, column, columns)
    stats[...] = columns.T[:16]
    links.send("stats", stats, stats_n, earlier)

    early_z[z] = collect("ex", early_x, group_steps).astype(BF16)
    spread_out("ez", early_z, z, z_steps)
    late_z[z] = collect("lx", late_x, group_steps)
    spread_out("lz", late_z, z, z_steps)
    early_y[y] = collect("ez", early_z, z_steps).astype(BF16)
    spread_out("ey", early_y, y, y_steps)

    links.arrived("query", query_n, earlier)
    links.arrived("stats", stats_n, earlier)
    links.arrived("grad", grad_context_n, earlier)
    for h in range(HEADS):
        query_h, grad_h = query_n[:, head(h)], grad_context_n[:, head(h)]
        scores = dot_nt(keys[:ROWS, head(h)], query_h) * SCALE + mask_next[...]
        share = jnp.exp(scores - stats_n[h : h + 1, :]) * stats_n[HEADS + h : HEADS + h + 1, :]
        grad_probs = dot_nt(values[:ROWS, head(h)], grad_h)
        grad_scores = (share * (grad_probs - stats_n[2 * HEADS + h : 2 * HEADS + h + 1, :]) * SCALE).astype(BF16)
        grad_key[:ROWS, head(h)] = dot(grad_scores, query_h).astype(BF16)
        grad_value[:ROWS, head(h)] = dot(share.astype(BF16), grad_h).astype(BF16)

    late_y[y] = collect("lz", late_z, z_steps)
    spread_out("ly", late_y, y, y_steps)
    early_all[group] = collect("ey", early_y, y_steps).astype(BF16)
    spread_out("ea", early_all, group, group_steps)

    grad_norm_a[...] += dot_nt(grad_key[:ROWS], weights[0]) + dot_nt(grad_value[:ROWS], weights[2])

    @pl.loop(0, 4, unroll=True)
    def _(step):
        part_rows = pl.ds(pl.multiple_of(step * 32, 32), 32)
        grad, scaled = grad_norm_a[part_rows, :] * gain_a[...], scaled_a[part_rows, :]
        first = jnp.mean(grad, axis=-1, keepdims=True)
        second = jnp.mean(grad * scaled, axis=-1, keepdims=True)
        result = spread(inverse_a[part_rows, :]) * (grad - first - scaled * second)
        frames_out[part_rows, :] = grad_mid_norm[part_rows, :] + result

    out_copy = bring(frames_out, out_frames.at[0])
    links.finish()

    factor = 1.0 / math.sqrt(NX * 2 * 2 * (NY // 2) * NZ * ROWS)
    for step, _, _, source in group_steps:
        links.arrived(("ea", step), early_all.at[source], sibling)
    for tile in range(WIDTH // 128):
        sums[:, tile * 128 : (tile + 1) * 128] = early_all[tile].astype(F32) * factor
    summed = collect("ly", late_y, y_steps) * factor
    for tile in range(WIDTH // 128):
        sums[11:12, tile * 128 : (tile + 1) * 128] = summed[tile : tile + 1]
    bring(sums, out_sums).wait()
    out_copy.wait()


def finish_kernel(frames_in, sums, out_frames, out_att, out_conv, out_kernel, out_bias):
    out_frames[...] = frames_in[...]

    @pl.when(pl.program_id(0) == 0)
    def _():
        out_kernel[...] = sums[:TAPS]
        out_bias[...] = sums[9:10]
        out_conv[...] = sums[10:11]
        out_att[...] = sums[11:12]


def scratch():
    def buffer(*shape, dtype=F32):
        return pltpu.VMEM(shape, dtype)

    return [
        buffer(EXT, WIDTH, dtype=BF16),
        buffer(CONV, WIDTH, dtype=BF16),
        buffer(3, 16, WIDTH // 2, dtype=BF16),
        buffer(3, 16, WIDTH // 2, dtype=BF16),
        buffer(4, WIDTH, HEADS_WIDTH, dtype=BF16),
        buffer(1, WIDTH),
        buffer(1, WIDTH),
        buffer(TAPS, WIDTH),
        buffer(1, WIDTH),
        buffer(EXT, WIDTH, dtype=BF16),
        buffer(2 * ROWS, WIDTH),
        buffer(ROWS, 128),
        buffer(EXT, HEADS_WIDTH, dtype=BF16),
        buffer(EXT, HEADS_WIDTH, dtype=BF16),
        buffer(ROWS, HEADS_WIDTH, dtype=BF16),
        buffer(16, HEADS_WIDTH, dtype=BF16),
        buffer(ROWS, HEADS_WIDTH, dtype=BF16),
        buffer(HEADS, ROWS, 2 * ROWS),
        buffer(HEADS, 16, EXT, dtype=BF16),
        buffer(CONV, HEADS_WIDTH),
        buffer(CONV, WIDTH),
        buffer(CONV, WIDTH),
        buffer(CONV, 128),
        buffer(WIDTH // 128, CONV, 128),
        buffer(ROWS + 8, 128, dtype=jnp.int32),
        buffer(ROWS + 8, 128),
        buffer(ROWS, WIDTH),
        buffer(ROWS, WIDTH),
        buffer(ROWS, WIDTH, dtype=BF16),
        buffer(ROWS, HEADS_WIDTH, dtype=BF16),
        buffer(ROWS, HEADS_WIDTH, dtype=BF16),
        buffer(ROWS, HEADS_WIDTH, dtype=BF16),
        buffer(2 * ROWS, HEADS_WIDTH, dtype=BF16),
        buffer(2 * ROWS, HEADS_WIDTH, dtype=BF16),
        buffer(ROWS, WIDTH),
        buffer(ROWS, WIDTH),
        buffer(ROWS, 2 * ROWS),
        buffer(16, EXT),
        buffer(ROWS, ROWS),
        buffer(16, 128),
        buffer(16, 128),
        buffer(GROUP, 16, 128),
        buffer(GROUP, 16, 128, dtype=BF16),
        buffer(GROUP, 16, 128, dtype=BF16),
        buffer(NY, 16, 128, dtype=BF16),
        buffer(NZ, 16, 128, dtype=BF16),
        buffer(GROUP, 16, 128, dtype=BF16),
        buffer(8, 128),
        buffer(GROUP, 8, 128),
        buffer(NY, 8, 128),
        buffer(NZ, 8, 128),
        buffer(16, WIDTH),
        pltpu.SemaphoreType.DMA((SLOTS,)),
        pltpu.SemaphoreType.DMA((SLOTS,)),
        pltpu.SemaphoreType.DMA((16,)),
    ]


def shards(
    frames, cotangent, lengths, w_query, w_key, w_value, w_output, att_gain, conv_gain, kernel, conv_bias
):
    row = (1, WIDTH)
    anywhere = pl.BlockSpec(memory_space=pl.ANY)
    in_specs = [anywhere] * 11
    in_specs[2] = pl.BlockSpec(memory_space=pltpu.SMEM)
    frames_sum, sums = pl.pallas_call(
        block_kernel,
        out_shape=(
            jax.ShapeDtypeStruct(frames.shape, F32),
            jax.ShapeDtypeStruct((16, WIDTH), F32),
        ),
        in_specs=in_specs,
        out_specs=(anywhere,) * 2,
        scratch_shapes=scratch(),
        compiler_params=pltpu.CompilerParams(
            collective_id=0, has_side_effects=True, vmem_limit_bytes=63 << 20
        ),
        cost_estimate=pl.CostEstimate(
            flops=3 << 30, bytes_accessed=4 << 20, transcendentals=1 << 20
        ),
    )(
        frames, cotangent, lengths, w_query, w_key, w_value, w_output.T,
        att_gain.reshape(row), conv_gain.reshape(row), kernel, conv_bias.reshape(row),
    )
    steps = 2
    moving = pl.BlockSpec((1, ROWS // steps, WIDTH), lambda step: (0, step, 0))

    def fixed(rows):
        return pl.BlockSpec((rows, WIDTH), lambda step: (0, 0))

    grad_frames, grad_att, grad_conv, grad_kernel, grad_bias = pl.pallas_call(
        finish_kernel,
        grid=(steps,),
        out_shape=(
            jax.ShapeDtypeStruct(frames.shape, F32),
            jax.ShapeDtypeStruct(row, F32),
            jax.ShapeDtypeStruct(row, F32),
            jax.ShapeDtypeStruct(kernel.shape, F32),
            jax.ShapeDtypeStruct(row, F32),
        ),
        in_specs=[moving, fixed(16)],
        out_specs=(moving, fixed(1), fixed(1), fixed(TAPS), fixed(1)),
        compiler_params=pltpu.CompilerParams(vmem_limit_bytes=63 << 20),
    )(frames_sum, sums)
    return (
        grad_frames,
        grad_att.reshape(WIDTH),
        grad_conv.reshape(WIDTH),
        grad_kernel,
        grad_bias.reshape(WIDTH),
    )


def solution(mesh):
    return jax.shard_map(
        shards,
        mesh=mesh,
        in_specs=(
            P("dp", "ctx", None),
            P("dp", "ctx", None),
            P("dp", None),
            P("dp", None),
            P("dp", None),
            P("dp", None),
            P(None, "dp"),
            P(),
            P(),
            P(),
            P(),
        ),
        out_specs=(P("dp", "ctx", None), P(), P(), P(), P()),
        check_vma=False,
    )
```

```python
import math

import jax
import jax.numpy as jnp
from jax import lax
from jax.experimental import pallas as pl
from jax.experimental.pallas import tpu as pltpu
from jax.sharding import PartitionSpec as P

MESH = pl.DeviceIdType.MESH
NX, NY, NZ = 4, 8, 8
ROWS = 128
WIDTH = 1024
HEADS = 4
HEAD_DIM = 128
HEADS_WIDTH = HEADS * HEAD_DIM
LEFT = 128
TAPS = 9
RIM = 16
EXT = 2 * ROWS + 2 * RIM
CONV = ROWS + 16
DEEP = 64
GROUP = 8
EPSILON = 1e-05
FAR = -1e30
BEFORE = -(1 << 20)
SCALE = HEAD_DIM ** (-0.5)
SLOTS = 176
F32 = jnp.float32
BF16 = jnp.bfloat16

SHARDS = ((-1, 0), (1, 0), (2, 0), (0, 1), (-1, 1), (1, 1), (2, 1), (0, 0))
DIRECT_SHARDS, FAR_SHARDS, OWN = (4, 5, 0, 1), (6, 2), 7
LATER, HALVED, FORWARD = (0, 1, 3), (4, 5, 6, 2), ((4, 0), (5, 0), (6, 0))
RELAYED = {0: (2, 0), 1: (2, 1), 4: (6, 0), 5: (6, 1)}


class Links:
    def __init__(self, send_sems, recv_sems):
        self.send_sems, self.recv_sems = send_sems, recv_sems
        self.names, self.sent = {}, []

    def copy(self, name, source, target, device):
        slot = self.names.setdefault(name, len(self.names))
        assert slot < SLOTS
        return pltpu.make_async_remote_copy(
            src_ref=source,
            dst_ref=target,
            send_sem=self.send_sems.at[slot],
            recv_sem=self.recv_sems.at[slot],
            device_id=device,
            device_id_type=MESH,
        )

    def send(self, name, source, target, device):
        copy = self.copy(name, source, target, device)
        copy.start()
        self.sent.append(copy)

    def arrived(self, name, target, device):
        self.copy(name, target, target, device).wait_recv()

    def finish(self):
        for copy in self.sent:
            copy.wait_send()


def dot(left, right):
    return jnp.dot(left, right, preferred_element_type=F32)


def dot_nt(left, right):
    return lax.dot_general(left, right, (((1,), (1,)), ((), ())), preferred_element_type=F32)


def dot_tn(left, right):
    return lax.dot_general(left, right, (((0,), (0,)), ((), ())), preferred_element_type=F32)


def normalize(values):
    center = values - jnp.mean(values, axis=-1, keepdims=True)
    inverse = lax.rsqrt(jnp.mean(center * center, axis=-1, keepdims=True) + EPSILON)
    return center * inverse, inverse


def wide(column, width):
    return jnp.broadcast_to(column, (column.shape[0], width))


def spread(block):
    return jnp.concatenate([block] * (WIDTH // 128), axis=1)


def iota(shape, axis):
    return lax.broadcasted_iota(jnp.int32, shape, axis)


def block_kernel(
    frames, cotangent, lengths, w_query, w_key, w_value, w_output, att_gain, conv_gain, kernel, bias,
    out_frames, out_sums,
    xs, cts, rims_out, rims_in, weights, gain_a, gain_c, taps_ref, bias_ref,
    norm_b, scaled_a, inverse_a, keys, values, query, query_e, query_n, probs, probs_rim, context, mid,
    scaled_c, inverse_c, conv_in, age, grad_conv, grad_conv_in, grad_mid_norm, grad_mid_b,
    grad_context, grad_context_n, grad_query, grad_key, grad_value, grad_norm_a,
    frames_out, mask_main, mask_rim, mask_next, stats, stats_n,
    early, early_b, early_x, early_y, early_z, early_all, late_sum, late_x, late_y, late_z,
    sums,
    send_sems, recv_sems, local_sems,
):
    dp, ctx = lax.axis_index("dp"), lax.axis_index("ctx")
    pair = lax.div(dp, 2)
    core = dp - 2 * pair
    y_lo = lax.div(pair, NX)
    x = pair - NX * y_lo
    z = lax.div(ctx, NY // 2)
    y_hi = ctx - (NY // 2) * z
    y = 2 * y_hi + y_lo
    offset = ctx * ROWS
    group = x * 2 + core

    def wrap(value, step, size):
        moved = value + step
        if isinstance(step, int) and step < 0:
            return jnp.where(moved < 0, moved + size, moved)
        return jnp.where(moved >= size, moved - size, moved)

    def flip(bit, change):
        return 1 - bit if change else bit

    def at(px, p_hi, p_lo, pz, pc):
        return ((p_lo * NX + px) * 2 + pc, pz * (NY // 2) + p_hi)

    def frames_at(step):
        return (dp, wrap(ctx, step, NZ * NY // 2))

    sibling = at(x, y_hi, y_lo, z, 1 - core)
    y_below = jnp.where(y_hi + y_lo == 0, NY // 2 - 1, y_hi + y_lo - 1)
    right, left = at(wrap(x, 1, NX), y_hi, y_lo, z, core), at(wrap(x, -1, NX), y_hi, y_lo, z, core)
    y_above = wrap(y_hi, y_lo, NY // 2)
    corners_above = [at(wrap(x, step, NX), y_above, 1 - y_lo, z, core) for step in (-1, 1)]
    corners_below = [at(wrap(x, step, NX), y_below, 1 - y_lo, z, core) for step in (-1, 1)]
    below = at(x, y_below, 1 - y_lo, z, core)
    front, back = at(x, y_hi, y_lo, wrap(z, 1, NZ), core), at(x, y_hi, y_lo, wrap(z, -1, NZ), core)
    later, earlier, later_2 = frames_at(1), frames_at(-1), frames_at(2)

    group_steps, y_steps, z_steps = [], [], []
    for step in (2, 1, -1, 0):
        for change in (1, 0):
            if (step, change) != (0, 0):
                to, of = wrap(x, step, NX), wrap(x, -step, NX)
                pc = flip(core, change)
                group_steps.append(((step, change), to * 2 + pc, at(to, y_hi, y_lo, z, pc), of * 2 + pc))
    for step in (2, -1, 1, 0):
        for change in (1, 0):
            if (step, change) != (0, 0):
                to, of = wrap(y_hi, step, NY // 2), wrap(y_hi, -step, NY // 2)
                lo = flip(y_lo, change)
                y_steps.append(((step, change), to * 2 + lo, at(x, to, lo, z, core), of * 2 + lo))
    for step in (4, 3, -3, 2, -2, 1, -1):
        to, of = wrap(z, step, NZ), wrap(z, -step, NZ)
        z_steps.append((step, to, at(x, y_hi, y_lo, to, core), of))

    links = Links(send_sems, recv_sems)
    local = []

    def bring(source, target):
        copy = pltpu.make_async_copy(source, target, local_sems.at[len(local)])
        copy.start()
        local.append(copy)
        return copy

    barrier = pltpu.get_barrier_semaphore()
    peers = [step[2] for step in z_steps + y_steps + group_steps]
    peers += [later, earlier, later_2, frames_at(-2)]
    peers += corners_above + corners_below
    for peer in peers:
        pl.semaphore_signal(barrier, inc=1, device_id=peer, device_id_type=MESH)

    own_rows = pl.ds(pl.multiple_of(dp * DEEP, DEEP), DEEP)
    got_weights = [
        bring(source, weights.at[index, own_rows, :])
        for index, source in ((0, w_key), (1, w_query), (2, w_value), (3, w_output))
    ]
    got_frames = bring(frames.at[0], xs.at[pl.ds(0, ROWS), :])
    got_rest = [
        bring(cotangent.at[0], cts.at[pl.ds(0, ROWS), :]),
        bring(att_gain, gain_a),
        bring(conv_gain, gain_c),
        bring(kernel, taps_ref),
        bring(bias, bias_ref),
    ]

    for copy in got_weights:
        copy.wait()
    got_frames.wait()
    for copy in got_rest:
        copy.wait()

    def pack(rows):
        return jnp.concatenate([rows[:, : WIDTH // 2], rows[:, WIDTH // 2 :]], axis=0).astype(BF16)

    def unpack(packed):
        rows = packed.astype(F32)
        return jnp.concatenate([rows[:8], rows[8:]], axis=1)

    rims_out[0] = pack(xs[ROWS - RIM : ROWS, :].astype(F32)[8:])
    rims_out[1] = pack(xs[:RIM, :].astype(F32)[:8])
    rims_out[2] = pack(cts[:RIM, :].astype(F32)[:8])
    pl.semaphore_wait(barrier, len(peers))

    half = z - 2 * lax.div(z, 2)

    def shard(index, of_core):
        step, other = SHARDS[index]
        return (flip(y_lo, other) * NX + wrap(x, step, NX)) * 2 + of_core

    def piece(index, of_half, part, wave, of_core):
        first, size = shard(index, of_core) * DEEP, DEEP
        if of_half is not None:
            first, size = first + of_half * 32, 32
        if part is not None:
            first, size = first + part * 16, 16
        return weights.at[:, pl.ds(pl.multiple_of(first, 16), size), :]

    def give(name, index, of_half, part, wave, device):
        ref = piece(index, of_half, part, wave, core)
        links.send((name, wave), ref, ref, device)

    def take(name, index, of_half, part, wave, of_core=None):
        ref = piece(index, of_half, part, wave, core if of_core is None else of_core)
        links.arrived((name, wave), ref, sibling)

    siblings = []

    def pass_on(name, index, of_half, part, wave):
        give("sib" + name, index, of_half, part, wave, sibling)
        siblings.append((name, index, of_half, part, wave))

    targets = {0: right, 1: left, 3: below, 4: corners_below[1], 5: corners_below[0]}

    def give_own(wave):
        for index in DIRECT_SHARDS:
            ref = piece(OWN, half, None, wave, core)
            links.send((str(index), wave), ref, ref, targets[index])
        pass_on("own", OWN, None, None, wave)

    give_own(0)

    links.send("prev2", rims_out.at[0], rims_in.at[0], later_2)
    links.send("next", rims_out.at[1], rims_in.at[1], earlier)
    links.send("cot", rims_out.at[2], rims_in.at[2], earlier)
    links.send("prev", frames.at[0], xs.at[pl.ds(ROWS, ROWS), :], later)

    def norm_rows(first, size, own):
        block = xs[pl.ds(first, size), :].astype(F32)
        scaled, inverse = normalize(block)
        norm_b[pl.ds(first, size), :] = (scaled * gain_a[...]).astype(BF16)
        if own is not None:
            scaled_a[pl.ds(first, size), :] = scaled
        if own:
            inverse_a[pl.ds(first, size), :] = wide(inverse, 128)
            mid[pl.ds(pl.multiple_of(first + 8, 8), size), :] = block
        return block

    @pl.loop(0, 4, unroll=True)
    def _(step):
        norm_rows(pl.multiple_of(step * 32, 32), 32, True)

    ends = [jnp.int32(0)]
    for record in range(lengths.shape[1]):
        ends.append(ends[-1] + lengths[0, record])

    def start_of(places):
        start = jnp.full(places.shape, BEFORE, jnp.int32)
        for end in ends:
            start = jnp.where(places >= end, end, start)
        return start

    def mask_of(query_places, key_places):
        first = jnp.maximum(start_of(query_places), query_places - LEFT)
        return jnp.where((key_places <= query_places) & (key_places >= first), 0.0, FAR).astype(F32)

    square = (ROWS, ROWS)
    place_rows, place_lanes = offset + iota(square, 0), offset + iota(square, 1)
    mask_main[:, :ROWS] = mask_of(place_rows, place_lanes)
    mask_main[:, ROWS:] = mask_of(place_rows, place_lanes - ROWS)
    mask_next[...] = mask_of(place_lanes + ROWS, place_rows)
    rim_rows = iota((16, EXT), 0)
    rim_places = offset + jnp.where(rim_rows < 8, rim_rows - 8, rim_rows + (ROWS - 8))
    lanes = iota((16, EXT), 1)
    rim_keys = jnp.where(lanes < ROWS, lanes, lanes - 2 * ROWS)
    rim_keys = jnp.where(lanes < 2 * ROWS, rim_keys, lanes - (3 * ROWS + RIM))
    rim_keys = offset + jnp.where(lanes < 2 * ROWS + RIM, rim_keys, lanes - (ROWS + RIM))
    mask_rim[...] = mask_of(rim_places, rim_keys)
    age_rows = offset + iota((ROWS + 8, 128), 0)
    age[...] = age_rows - start_of(age_rows)


    def pass_z(index, part, wave):
        give(f"z{part}{index}", index, half, part, wave, front if (index, part) in FORWARD else back)

    for wave in (0,):
        for index in DIRECT_SHARDS:
            take(str(index), index, half, None, wave)
            if index in RELAYED:
                further, part = RELAYED[index]
                give(f"{further}{part}", index, half, part, wave, (right, left)[part])
            if index in HALVED:
                for part in (0, 1):
                    pass_z(index, part, wave)
            pass_on(str(index), index, half, None, wave)
        for index in LATER:
            of_half = None if index == 3 else 1 - half
            ref = piece(OWN, of_half, None, wave, core)
            links.send((f"o{index}", wave), ref, ref, targets[index])
    for wave in (0,):
        for index in FAR_SHARDS:
            for part in (0, 1):
                take(f"{index}{part}", index, half, part, wave)
                pass_z(index, part, wave)
                pass_on(f"{index}{part}", index, half, part, wave)

    def take_rest(wave):
        for index in LATER:
            of_half = None if index == 3 else 1 - half
            take(f"o{index}", index, of_half, None, wave)
            pass_on(f"o{index}", index, of_half, None, wave)
        for index in HALVED:
            for part in (0, 1):
                take(f"z{part}{index}", index, 1 - half, part, wave)
                pass_on(f"z{part}{index}", index, 1 - half, part, wave)

    def take_siblings(of_wave):
        for name, index, of_half, part, wave in siblings:
            if wave == of_wave:
                take("sib" + name, index, of_half, part, wave, 1 - core)

    take_rest(0)

    links.arrived("prev", xs.at[pl.ds(ROWS, ROWS), :], earlier)
    links.arrived("prev2", rims_in.at[0], earlier)
    links.arrived("next", rims_in.at[1], earlier)
    links.arrived("cot", rims_in.at[2], earlier)
    zeros = jnp.zeros((8, WIDTH), F32)
    before, after, cot_after = (unpack(rims_in[index]) for index in range(3))
    xs[2 * ROWS : 2 * ROWS + RIM, :] = jnp.concatenate([zeros, before], axis=0).astype(BF16)
    xs[2 * ROWS + RIM :, :] = jnp.concatenate([after, zeros], axis=0).astype(BF16)
    cts[ROWS:, :] = jnp.concatenate([cot_after, zeros], axis=0).astype(BF16)

    @pl.loop(4, 8, unroll=True)
    def _(step):
        norm_rows(pl.multiple_of(step * 32, 32), 32, False)

    block = norm_rows(2 * ROWS, 2 * RIM, None)
    mid[pl.ds(ROWS + 8, 8), :] = block[RIM : RIM + 8]
    mid[pl.ds(0, 8), :] = xs[pl.ds(2 * ROWS - RIM, RIM), :].astype(F32)[8:]

    take_siblings(0)

    normed = norm_b[...]
    keys[...] = dot(normed, weights[0]).astype(BF16)
    rows = jnp.concatenate(
        [normed[:ROWS], normed[2 * ROWS - RIM : 2 * ROWS], normed[2 * ROWS + RIM :]], axis=0
    )
    projected = dot(rows, weights[1])
    query[...] = projected[:ROWS].astype(BF16)
    query_e[...] = projected[ROWS + 8 : ROWS + 24].astype(BF16)
    links.send("query", query, query_n, earlier)

    def head(index):
        return slice(index * HEAD_DIM, (index + 1) * HEAD_DIM)

    tops, shares = [], []
    for h in range(HEADS):
        scores = dot_nt(query[:, head(h)], keys[: 2 * ROWS, head(h)]) * SCALE + mask_main[...]
        top = jnp.max(scores, axis=-1, keepdims=True)
        shifted = jnp.exp(scores - top)
        part = 1.0 / jnp.sum(shifted, axis=-1, keepdims=True)
        probs[h] = shifted * part
        tops.append(top)
        shares.append(part)
        scores = dot_nt(query_e[:, head(h)], keys[:, head(h)]) * SCALE + mask_rim[...]
        shifted = jnp.exp(scores - jnp.max(scores, axis=-1, keepdims=True))
        share = shifted * (1.0 / jnp.sum(shifted, axis=-1, keepdims=True))
        probs_rim[h] = share.astype(BF16)
    values[...] = dot(norm_b[...], weights[2]).astype(BF16)
    for h in range(HEADS):
        context[8 : ROWS + 8, head(h)] = dot(probs[h].astype(BF16), values[: 2 * ROWS, head(h)])
        rims = dot(probs_rim[h], values[:, head(h)])
        context[0:8, head(h)] = rims[:8]
        context[ROWS + 8 :, head(h)] = rims[8:]

    mid[...] += dot_nt(context[...].astype(BF16), weights[3])

    @pl.loop(0, 3, unroll=True)
    def _(step):
        part_rows = pl.ds(pl.multiple_of(step * 48, 8), 48)
        scaled, inverse = normalize(mid[part_rows, :])
        scaled_c[part_rows, :] = scaled
        inverse_c[part_rows, :] = wide(inverse, 128)
        normed = (scaled * gain_c[...]).astype(BF16).astype(F32)
        for tile in range(WIDTH // 128):
            conv_in[tile, part_rows, :] = normed[:, tile * 128 : (tile + 1) * 128]

    @pl.loop(0, WIDTH // 128)
    def _(tile):
        part_lanes = pl.ds(pl.multiple_of(tile * 128, 128), 128)
        conv = jnp.broadcast_to(bias_ref[:, part_lanes], (ROWS + 8, 128))
        for back_by in range(TAPS):
            term = conv_in[tile, pl.ds(8 - back_by, ROWS + 8), :]
            term = term * taps_ref[TAPS - 1 - back_by : TAPS - back_by, part_lanes]
            conv = conv + jnp.where(age[...] >= back_by, term, 0.0)
        gate = 1.0 / (1.0 + jnp.exp(-conv))
        grad_out = cts[:, part_lanes].astype(F32)[: ROWS + 8]
        grad = grad_out * gate * (1.0 + conv * (1.0 - gate))
        grad_conv[...] = grad
        grad = grad[:ROWS]
        early[tile, 9:10, :] = jnp.sum(grad, axis=0, keepdims=True)
        total = jnp.zeros((ROWS, 128), F32)
        for back_by in range(TAPS):
            tap = TAPS - 1 - back_by
            kept = jnp.where(age[:ROWS, :] >= back_by, grad, 0.0)
            term = kept * conv_in[tile, pl.ds(8 - back_by, ROWS), :]
            early[tile, tap : tap + 1, :] = jnp.sum(term, axis=0, keepdims=True)
            ahead = pl.ds(back_by, ROWS)
            kept = jnp.where(age[ahead, :] >= back_by, grad_conv[ahead, :], 0.0)
            total = total + kept * taps_ref[tap : tap + 1, part_lanes]
        grad_conv_in[:, part_lanes] = total
        term = total * scaled_c[8 : ROWS + 8, part_lanes]
        early[tile, 10:11, :] = jnp.sum(term, axis=0, keepdims=True)
        early[tile, 11:16, :] = jnp.zeros((5, 128), F32)

    def spread_out(name, slots, me, steps):
        for step, _, device, _ in steps:
            links.send((name, step), slots.at[me], slots.at[me], device)

    def collect(name, slots, steps):
        for step, _, _, source in steps:
            links.arrived((name, step), slots.at[source], sibling)
        total = slots[0].astype(F32)
        for index in range(1, slots.shape[0]):
            total = total + slots[index].astype(F32)
        return total

    early_b[...] = early[...].astype(BF16)
    early_x[group] = early_b[group]
    for step, other, device, _ in group_steps:
        links.send(("ex", step), early_b.at[other], early_x.at[group], device)

    @pl.loop(0, 4, unroll=True)
    def _(step):
        part_rows = pl.ds(pl.multiple_of(step * 32, 32), 32)
        ext_rows = pl.ds(pl.multiple_of(step * 32 + 8, 8), 32)
        grad, scaled = grad_conv_in[part_rows, :] * gain_c[...], scaled_c[ext_rows, :]
        first = jnp.mean(grad, axis=-1, keepdims=True)
        second = jnp.mean(grad * scaled, axis=-1, keepdims=True)
        result = spread(inverse_c[ext_rows, :]) * (grad - first - scaled * second)
        grad_mid_norm[part_rows, :] = result
        grad_mid_b[part_rows, :] = (cts[part_rows, :].astype(F32) + result).astype(BF16)

    grad_context[...] = dot(grad_mid_b[...], weights[3]).astype(BF16)
    links.send("grad", grad_context, grad_context_n, earlier)
    deltas = []
    for h in range(HEADS):
        term = context[8 : ROWS + 8, head(h)] * grad_context[:, head(h)].astype(F32)
        deltas.append(jnp.sum(term, axis=-1, keepdims=True))

    for h in range(HEADS):
        grad_h = grad_context[:, head(h)]
        share = probs[h]
        grad_probs = dot_nt(grad_h, values[: 2 * ROWS, head(h)])
        grad_scores = (share * (grad_probs - deltas[h]) * SCALE).astype(BF16)
        grad_query[:, head(h)] = dot(grad_scores, keys[: 2 * ROWS, head(h)]).astype(BF16)
        grad_key[:, head(h)] = dot_tn(grad_scores, query[:, head(h)]).astype(BF16)
        grad_value[:, head(h)] = dot_tn(share.astype(BF16), grad_h).astype(BF16)

    parts = dot_nt(grad_key[...], weights[0]) + dot_nt(grad_value[...], weights[2])
    own_part = parts[:ROWS] + dot_nt(grad_query[...], weights[1])
    grad_norm_a[...] = own_part
    product = own_part * scaled_a[:ROWS] + parts[ROWS:] * scaled_a[ROWS:]
    total = jnp.sum(product, axis=0, keepdims=True)
    for tile in range(WIDTH // 128):
        late_sum[tile : tile + 1, :] = total[:, tile * 128 : (tile + 1) * 128]
    late_x[group] = late_sum[...]
    spread_out("lx", late_x, group, group_steps)

    lane = iota(square, 1)
    columns = jnp.zeros(square, F32)
    for index, column in enumerate(tops + shares + deltas):
        columns = jnp.where(lane == index, column, columns)
    stats[...] = columns.T[:16]
    links.send("stats", stats, stats_n, earlier)

    early_z[z] = collect("ex", early_x, group_steps).astype(BF16)
    spread_out("ez", early_z, z, z_steps)
    late_z[z] = collect("lx", late_x, group_steps)
    spread_out("lz", late_z, z, z_steps)
    early_y[y] = collect("ez", early_z, z_steps).astype(BF16)
    spread_out("ey", early_y, y, y_steps)

    links.arrived("query", query_n, earlier)
    links.arrived("stats", stats_n, earlier)
    links.arrived("grad", grad_context_n, earlier)
    for h in range(HEADS):
        query_h, grad_h = query_n[:, head(h)], grad_context_n[:, head(h)]
        scores = dot_nt(keys[:ROWS, head(h)], query_h) * SCALE + mask_next[...]
        share = jnp.exp(scores - stats_n[h : h + 1, :]) * stats_n[HEADS + h : HEADS + h + 1, :]
        grad_probs = dot_nt(values[:ROWS, head(h)], grad_h)
        grad_scores = (share * (grad_probs - stats_n[2 * HEADS + h : 2 * HEADS + h + 1, :]) * SCALE).astype(BF16)
        grad_key[:ROWS, head(h)] = dot(grad_scores, query_h).astype(BF16)
        grad_value[:ROWS, head(h)] = dot(share.astype(BF16), grad_h).astype(BF16)

    late_y[y] = collect("lz", late_z, z_steps)
    spread_out("ly", late_y, y, y_steps)
    early_all[group] = collect("ey", early_y, y_steps).astype(BF16)
    spread_out("ea", early_all, group, group_steps)

    grad_norm_a[...] += dot_nt(grad_key[:ROWS], weights[0]) + dot_nt(grad_value[:ROWS], weights[2])

    @pl.loop(0, 4, unroll=True)
    def _(step):
        part_rows = pl.ds(pl.multiple_of(step * 32, 32), 32)
        grad, scaled = grad_norm_a[part_rows, :] * gain_a[...], scaled_a[part_rows, :]
        first = jnp.mean(grad, axis=-1, keepdims=True)
        second = jnp.mean(grad * scaled, axis=-1, keepdims=True)
        result = spread(inverse_a[part_rows, :]) * (grad - first - scaled * second)
        frames_out[part_rows, :] = grad_mid_norm[part_rows, :] + result

    out_copy = bring(frames_out, out_frames.at[0])
    links.finish()

    factor = 1.0 / math.sqrt(NX * 2 * 2 * (NY // 2) * NZ * ROWS)
    for step, _, _, source in group_steps:
        links.arrived(("ea", step), early_all.at[source], sibling)
    for tile in range(WIDTH // 128):
        sums[:, tile * 128 : (tile + 1) * 128] = early_all[tile].astype(F32) * factor
    summed = collect("ly", late_y, y_steps) * factor
    for tile in range(WIDTH // 128):
        sums[11:12, tile * 128 : (tile + 1) * 128] = summed[tile : tile + 1]
    bring(sums, out_sums).wait()
    out_copy.wait()


def finish_kernel(frames_in, sums, out_frames, out_att, out_conv, out_kernel, out_bias):
    out_frames[...] = frames_in[...]

    @pl.when(pl.program_id(0) == 0)
    def _():
        out_kernel[...] = sums[:TAPS]
        out_bias[...] = sums[9:10]
        out_conv[...] = sums[10:11]
        out_att[...] = sums[11:12]


def scratch():
    def buffer(*shape, dtype=F32):
        return pltpu.VMEM(shape, dtype)

    return [
        buffer(EXT, WIDTH, dtype=BF16),
        buffer(CONV, WIDTH, dtype=BF16),
        buffer(3, 16, WIDTH // 2, dtype=BF16),
        buffer(3, 16, WIDTH // 2, dtype=BF16),
        buffer(4, WIDTH, HEADS_WIDTH, dtype=BF16),
        buffer(1, WIDTH),
        buffer(1, WIDTH),
        buffer(TAPS, WIDTH),
        buffer(1, WIDTH),
        buffer(EXT, WIDTH, dtype=BF16),
        buffer(2 * ROWS, WIDTH),
        buffer(ROWS, 128),
        buffer(EXT, HEADS_WIDTH, dtype=BF16),
        buffer(EXT, HEADS_WIDTH, dtype=BF16),
        buffer(ROWS, HEADS_WIDTH, dtype=BF16),
        buffer(16, HEADS_WIDTH, dtype=BF16),
        buffer(ROWS, HEADS_WIDTH, dtype=BF16),
        buffer(HEADS, ROWS, 2 * ROWS),
        buffer(HEADS, 16, EXT, dtype=BF16),
        buffer(CONV, HEADS_WIDTH),
        buffer(CONV, WIDTH),
        buffer(CONV, WIDTH),
        buffer(CONV, 128),
        buffer(WIDTH // 128, CONV, 128),
        buffer(ROWS + 8, 128, dtype=jnp.int32),
        buffer(ROWS + 8, 128),
        buffer(ROWS, WIDTH),
        buffer(ROWS, WIDTH),
        buffer(ROWS, WIDTH, dtype=BF16),
        buffer(ROWS, HEADS_WIDTH, dtype=BF16),
        buffer(ROWS, HEADS_WIDTH, dtype=BF16),
        buffer(ROWS, HEADS_WIDTH, dtype=BF16),
        buffer(2 * ROWS, HEADS_WIDTH, dtype=BF16),
        buffer(2 * ROWS, HEADS_WIDTH, dtype=BF16),
        buffer(ROWS, WIDTH),
        buffer(ROWS, WIDTH),
        buffer(ROWS, 2 * ROWS),
        buffer(16, EXT),
        buffer(ROWS, ROWS),
        buffer(16, 128),
        buffer(16, 128),
        buffer(GROUP, 16, 128),
        buffer(GROUP, 16, 128, dtype=BF16),
        buffer(GROUP, 16, 128, dtype=BF16),
        buffer(NY, 16, 128, dtype=BF16),
        buffer(NZ, 16, 128, dtype=BF16),
        buffer(GROUP, 16, 128, dtype=BF16),
        buffer(8, 128),
        buffer(GROUP, 8, 128),
        buffer(NY, 8, 128),
        buffer(NZ, 8, 128),
        buffer(16, WIDTH),
        pltpu.SemaphoreType.DMA((SLOTS,)),
        pltpu.SemaphoreType.DMA((SLOTS,)),
        pltpu.SemaphoreType.DMA((16,)),
    ]


def shards(
    frames, cotangent, lengths, w_query, w_key, w_value, w_output, att_gain, conv_gain, kernel, conv_bias
):
    row = (1, WIDTH)
    anywhere = pl.BlockSpec(memory_space=pl.ANY)
    in_specs = [anywhere] * 11
    in_specs[2] = pl.BlockSpec(memory_space=pltpu.SMEM)
    frames_sum, sums = pl.pallas_call(
        block_kernel,
        out_shape=(
            jax.ShapeDtypeStruct(frames.shape, F32),
            jax.ShapeDtypeStruct((16, WIDTH), F32),
        ),
        in_specs=in_specs,
        out_specs=(anywhere,) * 2,
        scratch_shapes=scratch(),
        compiler_params=pltpu.CompilerParams(
            collective_id=0, has_side_effects=True, vmem_limit_bytes=63 << 20
        ),
        cost_estimate=pl.CostEstimate(
            flops=3 << 30, bytes_accessed=4 << 20, transcendentals=1 << 20
        ),
    )(
        frames, cotangent, lengths, w_query, w_key, w_value, w_output.T,
        att_gain.reshape(row), conv_gain.reshape(row), kernel, conv_bias.reshape(row),
    )
    steps = 2
    moving = pl.BlockSpec((1, ROWS // steps, WIDTH), lambda step: (0, step, 0))

    def fixed(rows):
        return pl.BlockSpec((rows, WIDTH), lambda step: (0, 0))

    grad_frames, grad_att, grad_conv, grad_kernel, grad_bias = pl.pallas_call(
        finish_kernel,
        grid=(steps,),
        out_shape=(
            jax.ShapeDtypeStruct(frames.shape, F32),
            jax.ShapeDtypeStruct(row, F32),
            jax.ShapeDtypeStruct(row, F32),
            jax.ShapeDtypeStruct(kernel.shape, F32),
            jax.ShapeDtypeStruct(row, F32),
        ),
        in_specs=[moving, fixed(16)],
        out_specs=(moving, fixed(1), fixed(1), fixed(TAPS), fixed(1)),
        compiler_params=pltpu.CompilerParams(vmem_limit_bytes=63 << 20),
    )(frames_sum, sums)
    return (
        grad_frames,
        grad_att.reshape(WIDTH),
        grad_conv.reshape(WIDTH),
        grad_kernel,
        grad_bias.reshape(WIDTH),
    )


def solution(mesh):
    return jax.shard_map(
        shards,
        mesh=mesh,
        in_specs=(
            P("dp", "ctx", None),
            P("dp", "ctx", None),
            P("dp", None),
            P("dp", None),
            P("dp", None),
            P("dp", None),
            P(None, "dp"),
            P(),
            P(),
            P(),
            P(),
        ),
        out_specs=(P("dp", "ctx", None), P(), P(), P(), P()),
        check_vma=False,
    )
```
